128 devices in a mesh: dp: 4 (over x), expert: 32 (over z, y, core).
Axes of the slice: x: 4, y: 4, z: 4, core: 2. Of those that a mesh axis runs over, the one named last changes fastest.
Arguments:
- tokens: bfloat16 [16384, 7168], P(('dp', 'expert')), may hold values from -6 to 6
- cotangents: bfloat16 [16384, 8, 2048], P(('dp', 'expert')), may hold values from -6 to 6
- routing: int32 [16384, 8], P(('dp', 'expert')), may hold values from 0 to 127, all different within a row; in each aligned block of 128 rows (0 to 127, 128 to 255, ...) at most 9 rows name the same one
- sketch_matrix: bfloat16 [64, 7168], replicated, may hold values from -6 to 6
Outputs:
- basis: bfloat16 [128, 64, 2048], P('expert', None, 'dp')
- adapter: float32 [128, 64, 7168], P('expert', None, 'dp')
The draws below stay inside these ranges and needn't reach their ends.
Inputs may be any that keep to these rules, and one draw needn't show every extreme that they name: `routing`: each row names 8 different experts. Among the 128 rows of one device no expert is named more than 9 times, and in every draw some expert is named exactly 9 times by the rows of some device. Every expert is named by at least 64 rows in all.
All inputs are finite; a program needn't handle non-finite values.
Results may differ from the reference program's by a relative error of at most 0.04.
Values may be sent and summed in bfloat16 or wider, within the bound.
No kernel may reach another device: no remote copies, remote signals or barrier semaphores. Data moves between devices by JAX's collectives and lax.ppermute only.
A program may use at most 192 MiB of HBM per device.

```python
import math
import jax
import jax.numpy as jnp
import numpy as np
from jax import lax

D = 7168
FF = 2048
RANK = 64
TOP = 8
POWER = 2
TOK_DEV = 128
EXPERTS = 128
TOKENS = 16384
CAPACITY = 9
ROUTED = 1024
N_DP = 4
N_EXPERT = 32


def block_levels(own_key, shape, shards, low, top_value):
    level, own = 1.0, jax.random.fold_in(own_key, 6)
    for axis_at, blocks in shards:
        draws = jnp.exp(jax.random.uniform(jax.random.fold_in(own, axis_at), (blocks,), jnp.float32, low / len(shards), top_value / len(shards)))
        level = level * jnp.repeat(draws, shape[axis_at] // blocks).reshape([-1 if axis == axis_at else 1 for axis in range(len(shape))])
    return level


def assign_block(rng, own, number, rows, number_of, top, limit, lean):
    order = jax.random.permutation(rng, number_of)
    heavy_load, ordinary = portions_of(number_of, rows * top, limit, lean, True), portions_of(number_of, rows * top, limit, lean, False)
    places = jnp.arange(number_of)

    def named(lengths, rotation):
        used = int((lengths > 0).sum())
        fixed = max(1, used // 4)
        moved = fixed + (places - fixed + rotation * (used - fixed)) % max(1, number_of - fixed)
        return jnp.zeros((number_of,), jnp.int32).at[order[jnp.where(places < fixed, places, moved)]].set(jnp.asarray(lengths, jnp.int32))

    lengths = jnp.where(number % 4 == 0, named(heavy_load, number // 4), named(ordinary, number - number // 4 - 1))
    mixed = jax.random.permutation(jax.random.fold_in(own, 3), number_of)
    source_of, sink = mixed[0:number_of // 2 * 2:2], mixed[1:number_of // 2 * 2:2]
    margin = jnp.minimum(lengths[source_of] - 1, limit - lengths[sink]) // 2
    margin = jnp.where((source_of == order[0]) | (sink == order[0]) | (lengths[sink] == 0), 0, jnp.maximum(margin, 0))
    moved = jax.random.randint(jax.random.fold_in(own, 4), (number_of // 2,), 0, 1 << 20) % (margin + 1)
    lengths = lengths.at[source_of].add(-moved).at[sink].add(moved)
    labels = jnp.searchsorted(jnp.cumsum(lengths), jnp.arange(rows * top), side="right").astype(jnp.int32)
    table = labels.reshape(top, rows).T
    table = table[jax.random.permutation(jax.random.fold_in(own, 1), rows)]
    rotation = jax.random.randint(jax.random.fold_in(own, 2), (rows, 1), 0, top)
    return jnp.take_along_axis(table, (jnp.arange(top)[None, :] + rotation) % top, axis=1)


def portions_of(number_of, total, limit, slope, full):
    loads = [(1 << 20) // math.isqrt(rank ** slope) + 1 for rank in range(1, number_of + 1)]
    largest = limit if full else min(limit, max(-(-total // number_of), total * loads[0] // sum(loads)))
    least = 1 if total - largest >= number_of - 1 else 0
    given, spare = [largest] + [least] * (number_of - 1), total - largest - least * (number_of - 1)
    while spare > 0:
        movable = [i for i in range(1, number_of) if given[i] < largest] or [i for i in range(1, number_of) if given[i] < limit]
        whole, budget = sum([loads[i] for i in movable]), spare
        for i in movable:
            addition = min(limit - given[i], max(1, budget * loads[i] // whole), spare)
            given[i] = given[i] + addition
            spare = spare - addition
    return np.array(given)


def noise(rng, dims, deviation, reach, pieces=(), held_as=jnp.bfloat16):
    drawn = jax.random.normal(rng, dims, jnp.float32) * deviation
    if len(pieces) > 0:
        drawn = block_levels(rng, dims, pieces, -0.22, 0.18) * drawn
    return jnp.clip(drawn, min=-reach, max=reach).astype(held_as)


def setup_inputs(seed: int = 0) -> dict:
    streams_of = jax.random.split(jax.random.key(seed), 5)
    tokens = noise(streams_of[0], (TOKENS, D), 1.0, 6.0, ((0, 128),))
    cotangents = noise(streams_of[1], (TOKENS, TOP, FF), 1.0, 6.0, ((0, 128),))
    routing_keys = jax.random.split(jax.random.fold_in(streams_of[2], 1), TOKENS // TOK_DEV)
    routing_turns = jax.random.permutation(jax.random.fold_in(streams_of[2], 3), TOKENS // TOK_DEV)
    routing = jax.vmap(lambda own, number: assign_block(jax.random.fold_in(streams_of[2], 2), own, number, TOK_DEV, EXPERTS, TOP, CAPACITY, 1))(routing_keys, routing_turns).reshape((TOKENS, TOP))
    sketch_matrix = noise(streams_of[3], (RANK, D), 1.0, 6.0)
    return {"tokens": tokens, "cotangents": cotangents, "routing": routing, "sketch_matrix": sketch_matrix}


RIDGE_SHIFT = 0.0001

def slot_table(flat_ids, experts, capacity):
    routed_count = flat_ids.shape[0]
    onehot = (flat_ids[:, None] == jnp.arange(experts, dtype=jnp.int32)[None, :]).astype(jnp.int32)
    before = jnp.cumsum(onehot, axis=0) - onehot
    position = lax.optimization_barrier(jnp.sum(before * onehot, axis=1))
    target = flat_ids * capacity + position
    vacant = jnp.full((experts * capacity,), -1, jnp.int32)
    return vacant.at[target].set(jnp.arange(routed_count, dtype=jnp.int32))

def orthonormal(sketch):
    gram_matrix = jnp.dot(sketch, sketch.T, precision=lax.Precision.HIGHEST) / FF
    rank_size = gram_matrix.shape[0]
    diag_sum = jnp.trace(gram_matrix)
    shifted = gram_matrix + RIDGE_SHIFT * diag_sum / rank_size * jnp.eye(rank_size, dtype=gram_matrix.dtype)
    factor = jnp.linalg.cholesky(shifted)
    return lax.linalg.triangular_solve(factor, sketch, left_side=True, lower=True)

def reference(tokens, cotangents, routing, sketch_matrix):
    block_count = N_DP * N_EXPERT
    per_block = TOK_DEV * TOP
    tables = jax.vmap(lambda flat_ids: slot_table(flat_ids, EXPERTS, CAPACITY))(routing.reshape(block_count, per_block))
    offsets = (jnp.arange(block_count, dtype=jnp.int32) * per_block)[:, None]
    tables = jnp.where(tables >= 0, tables + offsets, -1)
    tables = tables.reshape(block_count, EXPERTS, CAPACITY).transpose(1, 0, 2)
    sketched = jnp.dot(tokens.astype(jnp.float32), sketch_matrix.T.astype(jnp.float32), preferred_element_type=jnp.float32).astype(jnp.bfloat16)
    flat_grads = cotangents.reshape(TOKENS * TOP, FF)
    adapter_scale = 1.0 / math.sqrt(FF * ROUTED)

    def per_expert(slot_index):
        present = (slot_index >= 0)[:, :, None]
        safe_index = jnp.maximum(slot_index, 0)
        token_row = safe_index // TOP
        owner_tokens = jnp.where(present, tokens[token_row], 0).astype(jnp.float32)
        owner_grads = jnp.where(present, flat_grads[safe_index], 0).astype(jnp.float32)
        sketch_rows = jnp.where(present, sketched[token_row], 0).astype(jnp.float32)
        grouped_tokens = owner_tokens.reshape(N_DP, N_EXPERT, CAPACITY, D)
        for iteration in range(POWER + 1):
            sketch = jnp.einsum('bcr,bcf->rf', sketch_rows, owner_grads)
            basis_full = orthonormal(sketch).astype(jnp.bfloat16)
            projected = jnp.einsum('rf,bcf->bcr', basis_full.astype(jnp.float32), owner_grads).astype(jnp.bfloat16)
            projected = lax.optimization_barrier(projected).astype(jnp.float32)
            partial_value = jnp.einsum('gscr,gscd->grd', projected.reshape(N_DP, N_EXPERT, CAPACITY, RANK), grouped_tokens) * adapter_scale
            if iteration < POWER:
                rounded = lax.optimization_barrier(partial_value.astype(jnp.bfloat16)).astype(jnp.float32)
                coefficient = lax.optimization_barrier(jnp.sum(rounded, axis=0)).astype(jnp.bfloat16)
                coefficient = lax.optimization_barrier(coefficient).astype(jnp.float32)
                sketch_rows = jnp.einsum('bcd,rd->bcr', owner_tokens, coefficient).astype(jnp.bfloat16)
                sketch_rows = lax.optimization_barrier(sketch_rows).astype(jnp.float32)
        adapter = lax.optimization_barrier(jnp.sum(partial_value, axis=0))
        return (basis_full, adapter)
    basis, adapter = lax.map(per_expert, tables)
    return (basis, adapter)
```

```python
import functools
import math

import jax
import jax.numpy as jnp
from jax import lax
from jax.experimental import pallas as pl
from jax.experimental.pallas import tpu as pltpu
from jax.sharding import PartitionSpec as P

D = 7168
FF = 2048
RANK = 64
TOP = 8
POWER = 2
TOK_DEV = 128
EXPERTS = 128
ROUTED = 1024
SLOTS = 8
ROWS = EXPERTS * SLOTS
FOLD_D = D // SLOTS
FOLD_FF = FF // SLOTS
G_WIDTH = FF + FOLD_FF + 128
X_WIDTH = D + FOLD_D
RIDGE_SHIFT = 0.0001
SCALE = 1.0 / math.sqrt(FF * ROUTED)
VMEM = 56 * 1024 * 1024
F32 = jnp.float32
BF16 = jnp.bfloat16
HIGHEST = lax.Precision.HIGHEST


def dot(a, b, contract, precision=None):
    return lax.dot_general(
        a, b, ((contract[:1], contract[1:]), ((), ())), precision=precision, preferred_element_type=F32
    )


def iota(shape, axis):
    return lax.broadcasted_iota(jnp.int32, shape, axis)


def ones_where(mask):
    return jnp.where(mask, 1.0, 0.0).astype(F32).astype(BF16)


def pack_grads_kernel(flat_ref, by_choice_ref, tok_ref, sketch_ref, cot_ref, out_ref, sel_ref, fold_ref, tail_ref):
    square = (EXPERTS, TOK_DEV)
    owner = iota(square, 0)
    named = jnp.zeros(square, F32)
    for k in range(TOP):
        named = named + jnp.where(by_choice_ref[k : k + 1, :] == owner, 1.0, 0.0)
    earlier = ones_where(iota(square, 0) < iota(square, 1))
    before = dot(named.astype(BF16), earlier, (1, 0))
    slot = jnp.where(named > 0.0, before, -1.0)
    spread = ones_where(iota((ROWS, EXPERTS), 0) // SLOTS == iota((ROWS, EXPERTS), 1))
    row_slot = dot(spread, slot.astype(BF16), (1, 0))
    sel = ones_where(row_slot == (iota((ROWS, TOK_DEV), 0) % SLOTS).astype(F32))
    sel_last = ones_where(slot == float(SLOTS))
    sel_ref[:ROWS, :] = sel
    sel_ref[ROWS:, :] = sel_last
    sketched = dot(tok_ref[...], sketch_ref[...], (1, 1)).astype(BF16)
    tail_ref[:, :RANK] = dot(sel, sketched, (1, 0))
    tail_ref[:, RANK:] = jnp.zeros((ROWS, 128 - RANK), F32)
    last_rows = dot(sel_last, sketched, (1, 0))
    tail_ref[pl.ds(0, EXPERTS, stride=SLOTS), :] = jnp.concatenate(
        [tail_ref[pl.ds(0, EXPERTS, stride=SLOTS), :][:, :RANK], last_rows], axis=1
    )
    out_ref[:, FF + FOLD_FF :] = tail_ref[...].astype(BF16)
    pairs = (TOK_DEV, TOK_DEV * TOP)
    token_of = ones_where(iota(pairs, 1) // TOP == iota(pairs, 0))
    flat = flat_ref[...]
    whole = (ROWS, TOK_DEV * TOP)
    sel_pair = ones_where((dot(sel, token_of, (1, 0)) > 0.5) & (iota(whole, 0) // SLOTS == flat))
    out_ref[:, :FF] = dot(sel_pair, cot_ref[...], (1, 0)).astype(BF16)
    last_pair = ones_where((dot(sel_last, token_of, (1, 0)) > 0.5) & (iota((EXPERTS, ROWS), 0) == flat))
    last = dot(last_pair, cot_ref[...], (1, 0))
    for r in range(SLOTS):
        for h in range(FOLD_FF // 128):
            c = r * FOLD_FF + h * 128
            fold_ref[h, pl.ds(r, EXPERTS, stride=SLOTS), :] = last[:, c : c + 128]
    for h in range(FOLD_FF // 128):
        out_ref[:, FF + h * 128 : FF + (h + 1) * 128] = fold_ref[h].astype(BF16)


def pack_grads(flat, by_choice, tokens, sketch_matrix, cot):
    return pl.pallas_call(
        pack_grads_kernel,
        out_shape=(
            jax.ShapeDtypeStruct((ROWS, G_WIDTH), BF16),
            jax.ShapeDtypeStruct((ROWS + EXPERTS, TOK_DEV), BF16),
        ),
        scratch_shapes=[pltpu.VMEM((FOLD_FF // 128, ROWS, 128), F32), pltpu.VMEM((ROWS, 128), F32)],
        compiler_params=pltpu.CompilerParams(vmem_limit_bytes=VMEM),
        cost_estimate=pl.CostEstimate(flops=2 * ROWS * ROWS * FF, bytes_accessed=14_000_000, transcendentals=0),
        name="pack_grads",
    )(flat, by_choice, tokens, sketch_matrix, cot)


def pack_tokens_kernel(sel_ref, tok_ref, out_ref, fold_ref):
    step = pl.program_id(0)

    @pl.when(step < SLOTS)
    def _():
        out_ref[...] = dot(sel_ref[:ROWS, :], tok_ref[...], (1, 0)).astype(BF16)
        last = dot(sel_ref[ROWS:, :], tok_ref[...], (1, 0))
        for h in range(FOLD_D // 128):
            fold_ref[h, pl.ds(step, EXPERTS, stride=SLOTS), :] = last[:, h * 128 : (h + 1) * 128]

    @pl.when(step == SLOTS)
    def _():
        for h in range(FOLD_D // 128):
            out_ref[:, h * 128 : (h + 1) * 128] = fold_ref[h].astype(BF16)


def pack_tokens(sel, tokens):
    return pl.pallas_call(
        pack_tokens_kernel,
        grid=(SLOTS + 1,),
        in_specs=[
            pl.BlockSpec((ROWS + EXPERTS, TOK_DEV), lambda i: (0, 0)),
            pl.BlockSpec((TOK_DEV, FOLD_D), lambda i: (0, jnp.minimum(i, SLOTS - 1))),
        ],
        out_specs=pl.BlockSpec((ROWS, FOLD_D), lambda i: (0, i)),
        out_shape=jax.ShapeDtypeStruct((ROWS, X_WIDTH), BF16),
        scratch_shapes=[pltpu.VMEM((FOLD_D // 128, ROWS, 128), F32)],
        compiler_params=pltpu.CompilerParams(vmem_limit_bytes=VMEM),
        cost_estimate=pl.CostEstimate(flops=2 * ROWS * TOK_DEV * D, bytes_accessed=19_000_000, transcendentals=0),
        name="pack_tokens",
    )(sel, tokens)


def inverse_factor(gram):
    rows, cols = iota((RANK, 2 * RANK), 0), iota((RANK, 2 * RANK), 1)
    diagonal = jnp.where(rows == cols, jnp.concatenate([gram, gram], axis=1), 0.0)
    mean = jnp.sum(jnp.sum(diagonal, axis=1, keepdims=True), axis=0, keepdims=True) / RANK
    unit = jnp.where(cols == rows + RANK, 1.0, 0.0)
    left = jnp.concatenate([gram, jnp.zeros((RANK, RANK), F32)], axis=1)
    work = left + unit + jnp.where(rows == cols, RIDGE_SHIFT * mean, 0.0)
    pivots = jnp.zeros((RANK, 1), F32)
    index = iota((RANK, 1), 0)
    for j in range(RANK):
        row = work[j : j + 1, :]
        pivot = row[:, j : j + 1]
        pivots = jnp.where(index == j, pivot, pivots)
        factor = jnp.where(index > j, work[:, j : j + 1] / pivot, 0.0)
        work = work - factor * row
    return work[:, RANK:] * lax.rsqrt(pivots)


def half_round(rows_main, rows_last, grads, grads_last):
    sketch = dot(rows_main, grads, (1, 0)) + dot(rows_last, grads_last, (1, 0))
    gram = dot(sketch, sketch, (1, 1), HIGHEST) / FF
    basis = dot(inverse_factor(gram), sketch, (1, 0), HIGHEST).astype(BF16)
    return basis, dot(basis, grads, (1, 1)).astype(BF16), dot(basis, grads_last, (1, 1)).astype(BF16)


def first_round_kernel(g_ref, main_ref, last_ref, grads_last_ref, fold_ref):
    for h in range(FOLD_FF // 128):
        fold_ref[h] = g_ref[:, FF + h * 128 : FF + (h + 1) * 128].astype(F32)
    for r in range(SLOTS):
        for h in range(FOLD_FF // 128):
            c = r * FOLD_FF + h * 128
            grads_last_ref[:, c : c + 128] = fold_ref[h, pl.ds(r, EXPERTS, stride=SLOTS), :].astype(BF16)
    fold_ref[0] = g_ref[:, FF + FOLD_FF :].astype(F32)
    tail_t = jnp.transpose(fold_ref[0])
    last_t = jnp.transpose(fold_ref[0, pl.ds(0, EXPERTS, stride=SLOTS), :])
    rows_main = tail_t[:RANK, :].astype(BF16)
    rows_last = last_t[RANK:, :].astype(BF16)
    _, main, last = half_round(rows_main, rows_last, g_ref[:, :FF], grads_last_ref[...])
    main_ref[...] = main
    last_ref[...] = last


def first_round(g):
    return pl.pallas_call(
        first_round_kernel,
        out_shape=(
            jax.ShapeDtypeStruct((RANK, ROWS), BF16),
            jax.ShapeDtypeStruct((RANK, EXPERTS), BF16),
            jax.ShapeDtypeStruct((EXPERTS, FF), BF16),
        ),
        scratch_shapes=[pltpu.VMEM((FOLD_FF // 128, ROWS, 128), F32)],
        compiler_params=pltpu.CompilerParams(vmem_limit_bytes=VMEM),
        cost_estimate=pl.CostEstimate(flops=20_000_000_000, bytes_accessed=6_000_000, transcendentals=0),
        name="first_round",
    )(g)


def power_kernel(x_hbm, g_hbm, main_ref, last_ref, grads_last_ref, basis_ref, adapter_ref, x_ref, x_last_ref, g_ref, fold_ref, sems):
    copies = []
    for i in range(SLOTS + 1):
        span = pl.ds(i * FOLD_D, FOLD_D)
        copies.append(pltpu.make_async_copy(x_hbm.at[:, span], x_ref.at[:, span], sems.at[i]))
    g_copy = pltpu.make_async_copy(g_hbm.at[:, pl.ds(0, FF)], g_ref, sems.at[SLOTS + 1])
    copies[SLOTS].start()
    for i in range(SLOTS):
        copies[i].start()
    g_copy.start()
    copies[SLOTS].wait()
    for h in range(FOLD_D // 128):
        fold_ref[h] = x_ref[:, D + h * 128 : D + (h + 1) * 128].astype(F32)
    for r in range(SLOTS):
        for h in range(FOLD_D // 128):
            c = r * FOLD_D + h * 128
            x_last_ref[:, c : c + 128] = fold_ref[h, pl.ds(r, EXPERTS, stride=SLOTS), :].astype(BF16)
    main, last = main_ref[...], last_ref[...]
    for step in range(POWER):
        rows_main = jnp.zeros((RANK, ROWS), F32)
        rows_last = jnp.zeros((RANK, EXPERTS), F32)
        for i in range(SLOTS):
            if step == 0:
                copies[i].wait()
            span = pl.ds(i * FOLD_D, FOLD_D)
            coefficient = dot(main, x_ref[:, span], (1, 0)) + dot(last, x_last_ref[:, span], (1, 0))
            coefficient = (coefficient * SCALE).astype(BF16)
            rows_main = rows_main + dot(coefficient, x_ref[:, span], (1, 1))
            rows_last = rows_last + dot(coefficient, x_last_ref[:, span], (1, 1))
        if step == 0:
            g_copy.wait()
        basis, main, last = half_round(
            rows_main.astype(BF16), rows_last.astype(BF16), g_ref[...], grads_last_ref[...]
        )
    basis_ref[...] = basis
    for i in range(SLOTS):
        span = pl.ds(i * FOLD_D, FOLD_D)
        adapter = dot(main, x_ref[:, span], (1, 0)) + dot(last, x_last_ref[:, span], (1, 0))
        adapter_ref[:, span] = (adapter * SCALE).astype(BF16)


def power(x, g, main, last, grads_last):
    anywhere, vmem = pl.BlockSpec(memory_space=pl.ANY), pl.BlockSpec(memory_space=pltpu.VMEM)
    return pl.pallas_call(
        power_kernel,
        in_specs=[anywhere, anywhere, vmem, vmem, vmem],
        out_specs=(vmem, vmem),
        out_shape=(jax.ShapeDtypeStruct((RANK, FF), BF16), jax.ShapeDtypeStruct((RANK, D), BF16)),
        scratch_shapes=[
            pltpu.VMEM((ROWS, X_WIDTH), BF16),
            pltpu.VMEM((EXPERTS, D), BF16),
            pltpu.VMEM((ROWS, FF), BF16),
            pltpu.VMEM((FOLD_D // 128, ROWS, 128), F32),
            pltpu.SemaphoreType.DMA((SLOTS + 2,)),
        ],
        compiler_params=pltpu.CompilerParams(vmem_limit_bytes=VMEM),
        cost_estimate=pl.CostEstimate(flops=40_000_000_000, bytes_accessed=24_000_000, transcendentals=0),
        name="power",
    )(x, g, main, last, grads_last)


def shards(tokens, cotangents, routing, sketch_matrix):
    groups = lax.axis_size("expert")
    everyone = ("dp", "expert")
    per_group = EXPERTS // groups
    owner = (routing % per_group) * groups + routing // per_group
    g_send, sel = pack_grads(
        owner.reshape(1, -1), owner.T, tokens, sketch_matrix, cotangents.reshape(TOK_DEV * TOP, FF)
    )
    x_send = pack_tokens(sel, tokens)
    swap = lambda v: lax.all_to_all(
        v.reshape(EXPERTS, SLOTS, v.shape[1]), everyone, split_axis=0, concat_axis=0, tiled=True
    ).reshape(v.shape)
    g = swap(g_send)
    x_send, g = lax.optimization_barrier((x_send, g))
    x = swap(x_send)
    main, last, grads_last = first_round(g)
    basis, adapter = power(x, g, main, last, grads_last)
    data = lax.axis_size("dp")
    both = jnp.concatenate(
        [adapter.reshape(RANK, data, -1), basis.reshape(RANK, data, -1)], axis=2
    ).transpose(1, 0, 2)
    both = lax.all_to_all(both, "dp", split_axis=0, concat_axis=0, tiled=True)
    width = D // data
    return both[:, :, width:], both[:, :, :width].astype(F32)


def solution(mesh):
    in_specs = (
        P(("dp", "expert"), None),
        P(("dp", "expert"), None, None),
        P(("dp", "expert"), None),
        P(),
    )
    out_specs = (P("expert", None, "dp"), P("expert", None, "dp"))
    return jax.shard_map(shards, mesh=mesh, in_specs=in_specs, out_specs=out_specs, check_vma=False)
```

```python
import functools
import math

import jax
import jax.numpy as jnp
from jax import lax
from jax.experimental import pallas as pl
from jax.experimental.pallas import tpu as pltpu
from jax.sharding import PartitionSpec as P

D = 7168
FF = 2048
RANK = 64
TOP = 8
POWER = 2
TOK_DEV = 128
EXPERTS = 128
ROUTED = 1024
SLOTS = 8
ROWS = EXPERTS * SLOTS
FOLD_D = D // SLOTS
FOLD_FF = FF // SLOTS
X_WIDTH = D + FOLD_D
WIDTH = X_WIDTH + FF + FOLD_FF
G_CHUNK = 512
GROUP = 256
RIDGE_SHIFT = 0.0001
SCALE = 1.0 / math.sqrt(FF * ROUTED)
VMEM = 56 * 1024 * 1024
F32 = jnp.float32
BF16 = jnp.bfloat16
HIGHEST = lax.Precision.HIGHEST


def dot(a, b, contract, precision=None):
    return lax.dot_general(
        a, b, ((contract[:1], contract[1:]), ((), ())), precision=precision, preferred_element_type=F32
    )


def iota(shape, axis):
    return lax.broadcasted_iota(jnp.int32, shape, axis)


def ones_where(mask):
    return jnp.where(mask, 1.0, 0.0).astype(F32).astype(BF16)


def fold(rows, r, fold_ref):
    for h in range(rows.shape[1] // 128):
        fold_ref[h, pl.ds(r, EXPERTS, stride=SLOTS), :] = rows[:, h * 128 : (h + 1) * 128]


def unfold(packed_ref, start, width, rows_ref, fold_ref):
    for h in range(width // 128):
        fold_ref[h] = packed_ref[:, start + h * 128 : start + (h + 1) * 128].astype(F32)
    for r in range(SLOTS):
        for h in range(width // 128):
            c = r * width + h * 128
            rows_ref[:, c : c + 128] = fold_ref[h, pl.ds(r, EXPERTS, stride=SLOTS), :].astype(BF16)


def pack_kernel(per_group, routing_ref, tok_hbm, cot_hbm, out_hbm, tok_ref, cot_ref, out_ref, fold_ref, in_sems, out_sems):
    parts = [pl.ds(r * FOLD_D, FOLD_D) for r in range(SLOTS)]
    tok_copies = [
        pltpu.make_async_copy(tok_hbm.at[:, part], tok_ref.at[:, part], in_sems.at[r]) for r, part in enumerate(parts)
    ]
    for copy in tok_copies:
        copy.start()
    cot_copy = pltpu.make_async_copy(cot_hbm, cot_ref, in_sems.at[SLOTS])
    cot_copy.start()
    sent = []

    def send(start, width):
        span = pl.ds(start, width)
        copy = pltpu.make_async_copy(out_ref.at[:, span], out_hbm.at[:, span], out_sems.at[len(sent)])
        copy.start()
        sent.append(copy)

    expert = routing_ref[...]
    owner = (expert % per_group) * (EXPERTS // per_group) + expert // per_group
    square = (EXPERTS, TOK_DEV)
    device = iota(square, 0)
    named = jnp.zeros(square, F32)
    for k in range(TOP):
        named = named + jnp.where(owner[k : k + 1, :] == device, 1.0, 0.0)
    earlier = ones_where(iota(square, 0) < iota(square, 1))
    slot = jnp.where(named > 0.0, dot(named.astype(BF16), earlier, (1, 0)), -1.0)
    spread = ones_where(iota((ROWS, EXPERTS), 0) // SLOTS == iota((ROWS, EXPERTS), 1))
    row_slot = dot(spread, slot.astype(BF16), (1, 0))
    sel = ones_where(row_slot == (iota((ROWS, TOK_DEV), 0) % SLOTS).astype(F32))
    sel_last = ones_where(slot == float(SLOTS))
    for r, part in enumerate(parts):
        tok_copies[r].wait()
        out_ref[:, part] = dot(sel, tok_ref[:, part], (1, 0)).astype(BF16)
        send(r * FOLD_D, FOLD_D)
        fold(dot(sel_last, tok_ref[:, part], (1, 0)), r, fold_ref)
    for h in range(FOLD_D // 128):
        out_ref[:, D + h * 128 : D + (h + 1) * 128] = fold_ref[h].astype(BF16)
    send(D, FOLD_D)

    pairs = (TOK_DEV, TOK_DEV * TOP)
    token_of = ones_where(iota(pairs, 1) // TOP == iota(pairs, 0))
    choices = dot(owner.astype(F32).astype(BF16), token_of, (1, 0))
    place = iota(choices.shape, 1) % TOP == iota(choices.shape, 0)
    flat = jnp.sum(jnp.where(place, choices, 0.0), axis=0, keepdims=True)
    row_owner = (iota((ROWS, 1), 0) // SLOTS).astype(F32)
    sel_pair = ones_where((dot(sel, token_of, (1, 0)) > 0.5) & (row_owner == flat))
    last_owner = iota((EXPERTS, 1), 0).astype(F32)
    last_pair = ones_where((dot(sel_last, token_of, (1, 0)) > 0.5) & (last_owner == flat))
    cot_copy.wait()
    for c in range(0, FF, G_CHUNK):
        out_ref[:, X_WIDTH + c : X_WIDTH + c + G_CHUNK] = dot(sel_pair, cot_ref[:, c : c + G_CHUNK], (1, 0)).astype(BF16)
        send(X_WIDTH + c, G_CHUNK)
        rows = dot(last_pair, cot_ref[:, c : c + G_CHUNK], (1, 0))
        for r in range(c // FOLD_FF, (c + G_CHUNK) // FOLD_FF):
            fold(rows[:, r * FOLD_FF - c : (r + 1) * FOLD_FF - c], r, fold_ref)
    for h in range(FOLD_FF // 128):
        start = X_WIDTH + FF + h * 128
        out_ref[:, start : start + 128] = fold_ref[h].astype(BF16)
    send(X_WIDTH + FF, FOLD_FF)
    for copy in sent:
        copy.wait()


def pack(routing_t, tokens, cot, per_group):
    anywhere, vmem = pl.BlockSpec(memory_space=pl.ANY), pl.BlockSpec(memory_space=pltpu.VMEM)
    return pl.pallas_call(
        functools.partial(pack_kernel, per_group),
        in_specs=[vmem, anywhere, anywhere],
        out_specs=anywhere,
        out_shape=jax.ShapeDtypeStruct((ROWS, WIDTH), BF16),
        scratch_shapes=[
            pltpu.VMEM((TOK_DEV, D), BF16),
            pltpu.VMEM((TOK_DEV * TOP, FF), BF16),
            pltpu.VMEM((ROWS, WIDTH), BF16),
            pltpu.VMEM((FOLD_D // 128, ROWS, 128), F32),
            pltpu.SemaphoreType.DMA((SLOTS + 1,)),
            pltpu.SemaphoreType.DMA((SLOTS + FF // G_CHUNK + 2,)),
        ],
        compiler_params=pltpu.CompilerParams(vmem_limit_bytes=VMEM),
        cost_estimate=pl.CostEstimate(flops=8_000_000_000, bytes_accessed=28_000_000, transcendentals=0),
        name="pack",
    )(routing_t, tokens, cot)


def inverse_factor(gram):
    panel, wide = 16, 2 * RANK
    rows, cols = iota((RANK, wide), 0), iota((RANK, wide), 1)
    diagonal = jnp.where(rows == cols, jnp.concatenate([gram, gram], axis=1), 0.0)
    mean = jnp.sum(jnp.sum(diagonal, axis=1, keepdims=True), axis=0, keepdims=True) / RANK
    work = jnp.concatenate([gram, jnp.zeros((RANK, RANK), F32)], axis=1)
    work = work + jnp.where(cols == rows + RANK, 1.0, 0.0) + jnp.where(rows == cols, RIDGE_SHIFT * mean, 0.0)
    done = []
    for j in range(0, RANK, panel):
        height = RANK - j
        index = iota((height, wide), 0)
        columns = [jnp.broadcast_to(work[:, j + k : j + k + 1], (height, wide)) for k in range(panel)]
        pivots = jnp.zeros((panel, wide), F32)
        for k in range(panel):
            pivot = columns[k][k : k + 1, :]
            factor = jnp.where(index > k, columns[k] * (1.0 / pivot), 0.0)
            pivots = jnp.where(index[:panel] == k, pivot, pivots)
            for m in range(k + 1, panel):
                columns[m] = columns[m] - factor * columns[m][k : k + 1, :]
            work = work - factor * work[k : k + 1, :]
        done.append(work[:panel, RANK:] * lax.rsqrt(pivots)[:, RANK:])
        work = work[panel:]
    return jnp.concatenate(done, axis=0)


def rows_of(coefficient_of, x_ref, x_last_ref):
    span = lambda i: pl.ds(i * FOLD_D, FOLD_D)
    groups = [jnp.zeros((GROUP, RANK), F32) for _ in range(ROWS // GROUP)]
    last = jnp.zeros((EXPERTS, RANK), F32)
    for i in range(SLOTS):
        coefficient = coefficient_of(i)
        for b in range(ROWS // GROUP):
            groups[b] = groups[b] + dot(x_ref[b * GROUP : (b + 1) * GROUP, span(i)], coefficient, (1, 1))
        last = last + dot(x_last_ref[:, span(i)], coefficient, (1, 1))
    main = jnp.concatenate([jnp.transpose(group) for group in groups], axis=1)
    return main.astype(BF16), jnp.transpose(last).astype(BF16)


def half_round(rows_main, rows_last, grads, grads_last):
    sketch = dot(rows_main, grads, (1, 0)) + dot(rows_last, grads_last, (1, 0))
    gram = dot(sketch, sketch, (1, 1), HIGHEST) / FF
    basis = dot(inverse_factor(gram), sketch, (1, 0), HIGHEST).astype(BF16)
    return basis, dot(basis, grads, (1, 1)).astype(BF16), dot(basis, grads_last, (1, 1)).astype(BF16)


def rounds_kernel(data, packed_hbm, sketch_ref, out_ref, packed_ref, x_last_ref, grads_last_ref, fold_ref, sems):
    def copy_of(start, width, number):
        span = pl.ds(start, width)
        return pltpu.make_async_copy(packed_hbm.at[:, span], packed_ref.at[:, span], sems.at[number])

    x_copies = [copy_of(i * FOLD_D, FOLD_D, i) for i in range(SLOTS + 1)]
    g_copy = copy_of(X_WIDTH, FF + FOLD_FF, SLOTS + 1)
    for copy in [x_copies[SLOTS]] + x_copies[:SLOTS] + [g_copy]:
        copy.start()
    span = lambda i: pl.ds(i * FOLD_D, FOLD_D)
    x_ref = packed_ref.at[:, pl.ds(0, D)]

    def first_coefficient(i):
        x_copies[i].wait()
        return sketch_ref[:, span(i)]

    x_copies[SLOTS].wait()
    unfold(packed_ref, D, FOLD_D, x_last_ref, fold_ref)
    main, last = rows_of(first_coefficient, x_ref, x_last_ref)
    g_copy.wait()
    unfold(packed_ref, X_WIDTH + FF, FOLD_FF, grads_last_ref, fold_ref)
    grads, grads_last = packed_ref[:, X_WIDTH : X_WIDTH + FF], grads_last_ref[...]
    basis, main, last = half_round(main, last, grads, grads_last)
    partial = lambda i: (dot(main, x_ref[:, span(i)], (1, 0)) + dot(last, x_last_ref[:, span(i)], (1, 0))) * SCALE
    for _ in range(POWER):
        main, last = rows_of(lambda i: partial(i).astype(BF16), x_ref, x_last_ref)
        basis, main, last = half_round(main, last, grads, grads_last)
    width, share = D // data, FF // data
    for g in range(data):
        out_ref[g, :, width:] = basis[:, g * share : (g + 1) * share]
        cols = pl.ds(g * width, width)
        adapter = (dot(main, x_ref[:, cols], (1, 0)) + dot(last, x_last_ref[:, cols], (1, 0))) * SCALE
        out_ref[g, :, :width] = adapter.astype(BF16)


def rounds(packed, sketch_matrix, data):
    anywhere, vmem = pl.BlockSpec(memory_space=pl.ANY), pl.BlockSpec(memory_space=pltpu.VMEM)
    return pl.pallas_call(
        functools.partial(rounds_kernel, data),
        in_specs=[anywhere, vmem],
        out_specs=vmem,
        out_shape=jax.ShapeDtypeStruct((data, RANK, (D + FF) // data), BF16),
        scratch_shapes=[
            pltpu.VMEM((ROWS, WIDTH), BF16),
            pltpu.VMEM((EXPERTS, D), BF16),
            pltpu.VMEM((EXPERTS, FF), BF16),
            pltpu.VMEM((FOLD_D // 128, ROWS, 128), F32),
            pltpu.SemaphoreType.DMA((SLOTS + 2,)),
        ],
        compiler_params=pltpu.CompilerParams(vmem_limit_bytes=VMEM),
        cost_estimate=pl.CostEstimate(flops=40_000_000_000, bytes_accessed=24_000_000, transcendentals=0),
        name="rounds",
    )(packed, sketch_matrix)


def shards(tokens, cotangents, routing, sketch_matrix):
    per_group = EXPERTS // lax.axis_size("expert")
    data = lax.axis_size("dp")
    packed = pack(routing.T, tokens, cotangents.reshape(TOK_DEV * TOP, FF), per_group)
    packed = lax.all_to_all(
        packed.reshape(EXPERTS, SLOTS, WIDTH), ("dp", "expert"), split_axis=0, concat_axis=0, tiled=True
    ).reshape(ROWS, WIDTH)
    both = lax.all_to_all(rounds(packed, sketch_matrix, data), "dp", split_axis=0, concat_axis=0, tiled=True)
    width = D // data
    return both[:, :, width:], both[:, :, :width].astype(F32)


def solution(mesh):
    in_specs = (
        P(("dp", "expert"), None),
        P(("dp", "expert"), None, None),
        P(("dp", "expert"), None),
        P(),
    )
    out_specs = (P("expert", None, "dp"), P("expert", None, "dp"))
    return jax.shard_map(shards, mesh=mesh, in_specs=in_specs, out_specs=out_specs, check_vma=False)
```

```python
import functools
import math

import jax
import jax.numpy as jnp
from jax import lax
from jax.experimental import pallas as pl
from jax.experimental.pallas import tpu as pltpu
from jax.sharding import PartitionSpec as P

D = 7168
FF = 2048
RANK = 64
TOP = 8
POWER = 2
TOK_DEV = 128
EXPERTS = 128
ROUTED = 1024
SLOTS = 8
ROWS = EXPERTS * SLOTS
FOLD_D = D // SLOTS
FOLD_FF = FF // SLOTS
X_WIDTH = D + FOLD_D
WIDTH = X_WIDTH + FF + FOLD_FF
G_CHUNK = 512
X_CHUNK = 2 * FOLD_D
GROUP = 256
RIDGE_SHIFT = 0.0001
SCALE = 1.0 / math.sqrt(FF * ROUTED)
VMEM = 56 * 1024 * 1024
ROUNDS_VMEM = 36 * 1024 * 1024
F32 = jnp.float32
BF16 = jnp.bfloat16
HIGHEST = lax.Precision.HIGHEST


def dot(a, b, contract, precision=None):
    return lax.dot_general(
        a, b, ((contract[:1], contract[1:]), ((), ())), precision=precision, preferred_element_type=F32
    )


def iota(shape, axis):
    return lax.broadcasted_iota(jnp.int32, shape, axis)


def ones_where(mask):
    return jnp.where(mask, 1.0, 0.0).astype(F32).astype(BF16)


def fold(rows, r, fold_ref):
    for h in range(rows.shape[1] // 128):
        fold_ref[h, pl.ds(r, EXPERTS, stride=SLOTS), :] = rows[:, h * 128 : (h + 1) * 128]


def unfold(packed_ref, start, width, rows_ref, fold_ref):
    for h in range(width // 128):
        fold_ref[h] = packed_ref[:, start + h * 128 : start + (h + 1) * 128].astype(F32)
    for r in range(SLOTS):
        for h in range(width // 128):
            c = r * width + h * 128
            rows_ref[:, c : c + 128] = fold_ref[h, pl.ds(r, EXPERTS, stride=SLOTS), :].astype(BF16)


def pack_kernel(per_group, routing_ref, tok_hbm, cot_hbm, out_hbm, tok_ref, cot_ref, out_ref, fold_ref, in_sems, out_sems):
    parts = [pl.ds(c, X_CHUNK) for c in range(0, D, X_CHUNK)]
    tok_copies = [
        pltpu.make_async_copy(tok_hbm.at[:, part], tok_ref.at[:, part], in_sems.at[r]) for r, part in enumerate(parts)
    ]
    for copy in tok_copies:
        copy.start()
    cot_copy = pltpu.make_async_copy(cot_hbm, cot_ref, in_sems.at[len(parts)])
    cot_copy.start()
    sent = []

    def send(start, width):
        span = pl.ds(start, width)
        copy = pltpu.make_async_copy(out_ref.at[:, span], out_hbm.at[:, span], out_sems.at[len(sent)])
        copy.start()
        sent.append(copy)

    expert = routing_ref[...]
    owner = (expert % per_group) * (EXPERTS // per_group) + expert // per_group
    square = (EXPERTS, TOK_DEV)
    device = iota(square, 0)
    named = jnp.zeros(square, F32)
    for k in range(TOP):
        named = named + jnp.where(owner[k : k + 1, :] == device, 1.0, 0.0)
    earlier = ones_where(iota(square, 0) < iota(square, 1))
    slot = jnp.where(named > 0.0, dot(named.astype(BF16), earlier, (1, 0)), -1.0)
    spread = ones_where(iota((ROWS, EXPERTS), 0) // SLOTS == iota((ROWS, EXPERTS), 1))
    row_slot = dot(spread, slot.astype(BF16), (1, 0))
    sel = ones_where(row_slot == (iota((ROWS, TOK_DEV), 0) % SLOTS).astype(F32))
    sel_last = ones_where(slot == float(SLOTS))
    for r, part in enumerate(parts):
        tok_copies[r].wait()
        out_ref[:, part] = dot(sel, tok_ref[:, part], (1, 0)).astype(BF16)
        send(r * X_CHUNK, X_CHUNK)
        rows = dot(sel_last, tok_ref[:, part], (1, 0))
        for q in range(X_CHUNK // FOLD_D):
            fold(rows[:, q * FOLD_D : (q + 1) * FOLD_D], r * (X_CHUNK // FOLD_D) + q, fold_ref)
    for h in range(FOLD_D // 128):
        out_ref[:, D + h * 128 : D + (h + 1) * 128] = fold_ref[h].astype(BF16)
    send(D, FOLD_D)

    pairs = (TOK_DEV, TOK_DEV * TOP)
    token_of = ones_where(iota(pairs, 1) // TOP == iota(pairs, 0))
    choices = dot(owner.astype(F32).astype(BF16), token_of, (1, 0))
    place = iota(choices.shape, 1) % TOP == iota(choices.shape, 0)
    flat = jnp.sum(jnp.where(place, choices, 0.0), axis=0, keepdims=True)
    row_owner = (iota((ROWS, 1), 0) // SLOTS).astype(F32)
    sel_pair = ones_where((dot(sel, token_of, (1, 0)) > 0.5) & (row_owner == flat))
    last_owner = iota((EXPERTS, 1), 0).astype(F32)
    last_pair = ones_where((dot(sel_last, token_of, (1, 0)) > 0.5) & (last_owner == flat))
    cot_copy.wait()
    for c in range(0, FF, G_CHUNK):
        out_ref[:, X_WIDTH + c : X_WIDTH + c + G_CHUNK] = dot(sel_pair, cot_ref[:, c : c + G_CHUNK], (1, 0)).astype(BF16)
        send(X_WIDTH + c, G_CHUNK)
        rows = dot(last_pair, cot_ref[:, c : c + G_CHUNK], (1, 0))
        for r in range(c // FOLD_FF, (c + G_CHUNK) // FOLD_FF):
            fold(rows[:, r * FOLD_FF - c : (r + 1) * FOLD_FF - c], r, fold_ref)
    for h in range(FOLD_FF // 128):
        start = X_WIDTH + FF + h * 128
        out_ref[:, start : start + 128] = fold_ref[h].astype(BF16)
    send(X_WIDTH + FF, FOLD_FF)
    for copy in sent:
        copy.wait()


def pack(routing_t, tokens, cot, per_group):
    anywhere, vmem = pl.BlockSpec(memory_space=pl.ANY), pl.BlockSpec(memory_space=pltpu.VMEM)
    return pl.pallas_call(
        functools.partial(pack_kernel, per_group),
        in_specs=[vmem, anywhere, anywhere],
        out_specs=anywhere,
        out_shape=jax.ShapeDtypeStruct((ROWS, WIDTH), BF16),
        scratch_shapes=[
            pltpu.VMEM((TOK_DEV, D), BF16),
            pltpu.VMEM((TOK_DEV * TOP, FF), BF16),
            pltpu.VMEM((ROWS, WIDTH), BF16),
            pltpu.VMEM((FOLD_D // 128, ROWS, 128), F32),
            pltpu.SemaphoreType.DMA((D // X_CHUNK + 1,)),
            pltpu.SemaphoreType.DMA((D // X_CHUNK + FF // G_CHUNK + 2,)),
        ],
        compiler_params=pltpu.CompilerParams(vmem_limit_bytes=VMEM),
        cost_estimate=pl.CostEstimate(flops=8_000_000_000, bytes_accessed=28_000_000, transcendentals=0),
        name="pack",
    )(routing_t, tokens, cot)


def inverse_factor(gram):
    panel, wide = 16, 2 * RANK
    rows, cols = iota((RANK, wide), 0), iota((RANK, wide), 1)
    diagonal = jnp.where(rows == cols, jnp.concatenate([gram, gram], axis=1), 0.0)
    mean = jnp.sum(jnp.sum(diagonal, axis=1, keepdims=True), axis=0, keepdims=True) / RANK
    work = jnp.concatenate([gram, jnp.zeros((RANK, RANK), F32)], axis=1)
    work = work + jnp.where(cols == rows + RANK, 1.0, 0.0) + jnp.where(rows == cols, RIDGE_SHIFT * mean, 0.0)
    done = []
    for j in range(0, RANK, panel):
        height = RANK - j
        index = iota((height, wide), 0)
        columns = [jnp.broadcast_to(work[:, j + k : j + k + 1], (height, wide)) for k in range(panel)]
        pivots = jnp.zeros((panel, wide), F32)
        for k in range(panel):
            pivot = columns[k][k : k + 1, :]
            factor = jnp.where(index > k, columns[k] * (1.0 / pivot), 0.0)
            pivots = jnp.where(index[:panel] == k, pivot, pivots)
            for m in range(k + 1, panel):
                columns[m] = columns[m] - factor * columns[m][k : k + 1, :]
            work = work - factor * work[k : k + 1, :]
        done.append(work[:panel, RANK:] * lax.rsqrt(pivots)[:, RANK:])
        work = work[panel:]
    return jnp.concatenate(done, axis=0)


def rows_of(coefficient_of, x_ref, x_last_ref):
    span = lambda i: pl.ds(i * FOLD_D, FOLD_D)
    groups = [jnp.zeros((GROUP, RANK), F32) for _ in range(ROWS // GROUP)]
    last = jnp.zeros((EXPERTS, RANK), F32)
    for i in range(SLOTS):
        coefficient = coefficient_of(i)
        for b in range(ROWS // GROUP):
            groups[b] = groups[b] + dot(x_ref[b * GROUP : (b + 1) * GROUP, span(i)], coefficient, (1, 1))
        last = last + dot(x_last_ref[:, span(i)], coefficient, (1, 1))
    main = jnp.concatenate([jnp.transpose(group) for group in groups], axis=1)
    return main.astype(BF16), jnp.transpose(last).astype(BF16)


def half_round(rows_main, rows_last, grads, grads_last):
    sketch = (dot(rows_main, grads, (1, 0)) + dot(rows_last, grads_last, (1, 0))).astype(BF16)
    inverse = inverse_factor(dot(sketch, sketch, (1, 1)) / FF)
    main = dot(inverse, dot(sketch, grads, (1, 1)), (1, 0), HIGHEST)
    last = dot(inverse, dot(sketch, grads_last, (1, 1)), (1, 0), HIGHEST)
    return sketch, inverse, main.astype(BF16), last.astype(BF16)


def rounds_kernel(data, packed_ref, sketch_ref, out_ref, x_last_ref, grads_last_ref, fold_ref):
    span = lambda i: pl.ds(i * FOLD_D, FOLD_D)
    x_ref = packed_ref.at[:, pl.ds(0, D)]

    unfold(packed_ref, D, FOLD_D, x_last_ref, fold_ref)
    main, last = rows_of(lambda i: sketch_ref[:, span(i)], x_ref, x_last_ref)
    unfold(packed_ref, X_WIDTH + FF, FOLD_FF, grads_last_ref, fold_ref)
    grads, grads_last = packed_ref[:, X_WIDTH : X_WIDTH + FF], grads_last_ref[...]
    sketch, inverse, main, last = half_round(main, last, grads, grads_last)
    partial = lambda i: (dot(main, x_ref[:, span(i)], (1, 0)) + dot(last, x_last_ref[:, span(i)], (1, 0))) * SCALE
    for _ in range(POWER):
        main, last = rows_of(lambda i: partial(i).astype(BF16), x_ref, x_last_ref)
        sketch, inverse, main, last = half_round(main, last, grads, grads_last)
    basis = dot(inverse, sketch.astype(F32), (1, 0), HIGHEST).astype(BF16)
    width, share = D // data, FF // data
    for g in range(data):
        out_ref[g, :, width:] = basis[:, g * share : (g + 1) * share]
        cols = pl.ds(g * width, width)
        adapter = (dot(main, x_ref[:, cols], (1, 0)) + dot(last, x_last_ref[:, cols], (1, 0))) * SCALE
        out_ref[g, :, :width] = adapter.astype(BF16)


def rounds(packed, sketch_matrix, data):
    vmem = pl.BlockSpec(memory_space=pltpu.VMEM)
    return pl.pallas_call(
        functools.partial(rounds_kernel, data),
        in_specs=[vmem, vmem],
        out_specs=vmem,
        out_shape=jax.ShapeDtypeStruct((data, RANK, (D + FF) // data), BF16),
        scratch_shapes=[
            pltpu.VMEM((EXPERTS, D), BF16),
            pltpu.VMEM((EXPERTS, FF), BF16),
            pltpu.VMEM((FOLD_D // 128, ROWS, 128), F32),
        ],
        compiler_params=pltpu.CompilerParams(vmem_limit_bytes=ROUNDS_VMEM),
        cost_estimate=pl.CostEstimate(flops=40_000_000_000, bytes_accessed=24_000_000, transcendentals=0),
        name="rounds",
    )(packed, sketch_matrix)


def shards(tokens, cotangents, routing, sketch_matrix):
    per_group = EXPERTS // lax.axis_size("expert")
    data = lax.axis_size("dp")
    packed = pack(routing.T, tokens, cotangents.reshape(TOK_DEV * TOP, FF), per_group)
    packed = lax.all_to_all(
        packed.reshape(EXPERTS, SLOTS, WIDTH), ("dp", "expert"), split_axis=0, concat_axis=0, tiled=True
    ).reshape(ROWS, WIDTH)
    packed = pltpu.with_memory_space_constraint(packed, pltpu.VMEM)
    both = lax.all_to_all(rounds(packed, sketch_matrix, data), "dp", split_axis=0, concat_axis=0, tiled=True)
    width = D // data
    return both[:, :, width:], both[:, :, :width].astype(F32)


def solution(mesh):
    in_specs = (
        P(("dp", "expert"), None),
        P(("dp", "expert"), None, None),
        P(("dp", "expert"), None),
        P(),
    )
    out_specs = (P("expert", None, "dp"), P("expert", None, "dp"))
    return jax.shard_map(shards, mesh=mesh, in_specs=in_specs, out_specs=out_specs, check_vma=False)
```

```python
import functools
import math

import jax
import jax.numpy as jnp
from jax import lax
from jax.experimental import pallas as pl
from jax.experimental.pallas import tpu as pltpu
from jax.sharding import PartitionSpec as P

D = 7168
FF = 2048
RANK = 64
TOP = 8
POWER = 2
TOK_DEV = 128
EXPERTS = 128
ROUTED = 1024
SLOTS = 8
ROWS = EXPERTS * SLOTS
FOLD_D = D // SLOTS
FOLD_FF = FF // SLOTS
X_WIDTH = D + FOLD_D
WIDTH = X_WIDTH + FF + FOLD_FF
G_CHUNK = 512
X_CHUNK = 2 * FOLD_D
GROUP = 256
RIDGE_SHIFT = 0.0001
SCALE = 1.0 / math.sqrt(FF * ROUTED)
VMEM = 56 * 1024 * 1024
ROUNDS_VMEM = 36 * 1024 * 1024
F32 = jnp.float32
BF16 = jnp.bfloat16
HIGHEST = lax.Precision.HIGHEST


def dot(a, b, contract, precision=None):
    return lax.dot_general(
        a, b, ((contract[:1], contract[1:]), ((), ())), precision=precision, preferred_element_type=F32
    )


def iota(shape, axis):
    return lax.broadcasted_iota(jnp.int32, shape, axis)


def ones_where(mask):
    return jnp.where(mask, 1.0, 0.0).astype(F32).astype(BF16)


def fold(rows, r, fold_ref):
    for h in range(rows.shape[1] // 128):
        fold_ref[h, pl.ds(r, EXPERTS, stride=SLOTS), :] = rows[:, h * 128 : (h + 1) * 128]


def unfold(packed_ref, start, width, rows_ref, fold_ref):
    for h in range(width // 128):
        fold_ref[h] = packed_ref[:, start + h * 128 : start + (h + 1) * 128].astype(F32)
    for r in range(SLOTS):
        for h in range(width // 128):
            c = r * width + h * 128
            rows_ref[:, c : c + 128] = fold_ref[h, pl.ds(r, EXPERTS, stride=SLOTS), :].astype(BF16)


def pack_kernel(per_group, routing_ref, tok_hbm, cot_hbm, out_hbm, tok_ref, cot_ref, out_ref, fold_ref, in_sems, out_sems):
    parts = [pl.ds(c, X_CHUNK) for c in range(0, D, X_CHUNK)]
    tok_copies = [
        pltpu.make_async_copy(tok_hbm.at[:, part], tok_ref.at[:, part], in_sems.at[r]) for r, part in enumerate(parts)
    ]
    for copy in tok_copies:
        copy.start()
    cot_copy = pltpu.make_async_copy(cot_hbm, cot_ref, in_sems.at[len(parts)])
    cot_copy.start()
    sent = []

    def send(start, width):
        span = pl.ds(start, width)
        copy = pltpu.make_async_copy(out_ref.at[:, span], out_hbm.at[:, span], out_sems.at[len(sent)])
        copy.start()
        sent.append(copy)

    expert = routing_ref[...]
    owner = (expert % per_group) * (EXPERTS // per_group) + expert // per_group
    square = (EXPERTS, TOK_DEV)
    device = iota(square, 0)
    named = jnp.zeros(square, F32)
    for k in range(TOP):
        named = named + jnp.where(owner[k : k + 1, :] == device, 1.0, 0.0)
    earlier = ones_where(iota(square, 0) < iota(square, 1))
    slot = jnp.where(named > 0.0, dot(named.astype(BF16), earlier, (1, 0)), -1.0)
    spread = ones_where(iota((ROWS, EXPERTS), 0) // SLOTS == iota((ROWS, EXPERTS), 1))
    row_slot = dot(spread, slot.astype(BF16), (1, 0))
    sel = ones_where(row_slot == (iota((ROWS, TOK_DEV), 0) % SLOTS).astype(F32))
    sel_last = ones_where(slot == float(SLOTS))
    for r, part in enumerate(parts):
        tok_copies[r].wait()
        out_ref[:, part] = dot(sel, tok_ref[:, part], (1, 0)).astype(BF16)
        send(r * X_CHUNK, X_CHUNK)
        rows = dot(sel_last, tok_ref[:, part], (1, 0))
        for q in range(X_CHUNK // FOLD_D):
            fold(rows[:, q * FOLD_D : (q + 1) * FOLD_D], r * (X_CHUNK // FOLD_D) + q, fold_ref)
    for h in range(FOLD_D // 128):
        out_ref[:, D + h * 128 : D + (h + 1) * 128] = fold_ref[h].astype(BF16)
    send(D, FOLD_D)

    pairs = (TOK_DEV, TOK_DEV * TOP)
    token_of = ones_where(iota(pairs, 1) // TOP == iota(pairs, 0))
    choices = dot(owner.astype(F32).astype(BF16), token_of, (1, 0))
    place = iota(choices.shape, 1) % TOP == iota(choices.shape, 0)
    flat = jnp.sum(jnp.where(place, choices, 0.0), axis=0, keepdims=True)
    row_owner = (iota((ROWS, 1), 0) // SLOTS).astype(F32)
    sel_pair = ones_where((dot(sel, token_of, (1, 0)) > 0.5) & (row_owner == flat))
    last_owner = iota((EXPERTS, 1), 0).astype(F32)
    last_pair = ones_where((dot(sel_last, token_of, (1, 0)) > 0.5) & (last_owner == flat))
    cot_copy.wait()
    for c in range(0, FF, G_CHUNK):
        out_ref[:, X_WIDTH + c : X_WIDTH + c + G_CHUNK] = dot(sel_pair, cot_ref[:, c : c + G_CHUNK], (1, 0)).astype(BF16)
        send(X_WIDTH + c, G_CHUNK)
        rows = dot(last_pair, cot_ref[:, c : c + G_CHUNK], (1, 0))
        for r in range(c // FOLD_FF, (c + G_CHUNK) // FOLD_FF):
            fold(rows[:, r * FOLD_FF - c : (r + 1) * FOLD_FF - c], r, fold_ref)
    for h in range(FOLD_FF // 128):
        start = X_WIDTH + FF + h * 128
        out_ref[:, start : start + 128] = fold_ref[h].astype(BF16)
    send(X_WIDTH + FF, FOLD_FF)
    for copy in sent:
        copy.wait()


def pack(routing_t, tokens, cot, per_group):
    anywhere, vmem = pl.BlockSpec(memory_space=pl.ANY), pl.BlockSpec(memory_space=pltpu.VMEM)
    return pl.pallas_call(
        functools.partial(pack_kernel, per_group),
        in_specs=[vmem, anywhere, anywhere],
        out_specs=anywhere,
        out_shape=jax.ShapeDtypeStruct((ROWS, WIDTH), BF16),
        scratch_shapes=[
            pltpu.VMEM((TOK_DEV, D), BF16),
            pltpu.VMEM((TOK_DEV * TOP, FF), BF16),
            pltpu.VMEM((ROWS, WIDTH), BF16),
            pltpu.VMEM((FOLD_D // 128, ROWS, 128), F32),
            pltpu.SemaphoreType.DMA((D // X_CHUNK + 1,)),
            pltpu.SemaphoreType.DMA((D // X_CHUNK + FF // G_CHUNK + 2,)),
        ],
        compiler_params=pltpu.CompilerParams(vmem_limit_bytes=VMEM),
        cost_estimate=pl.CostEstimate(flops=8_000_000_000, bytes_accessed=28_000_000, transcendentals=0),
        name="pack",
    )(routing_t, tokens, cot)


def inverse_factor(gram):
    panel, wide = 16, 2 * RANK
    rows, cols = iota((RANK, wide), 0), iota((RANK, wide), 1)
    diagonal = jnp.where(rows == cols, jnp.concatenate([gram, gram], axis=1), 0.0)
    mean = jnp.sum(jnp.sum(diagonal, axis=1, keepdims=True), axis=0, keepdims=True) / RANK
    work = jnp.concatenate([gram, jnp.zeros((RANK, RANK), F32)], axis=1)
    work = work + jnp.where(cols == rows + RANK, 1.0, 0.0) + jnp.where(rows == cols, RIDGE_SHIFT * mean, 0.0)
    done = []
    for j in range(0, RANK, panel):
        height = RANK - j
        index = iota((height, wide), 0)
        columns = [jnp.broadcast_to(work[:, j + k : j + k + 1], (height, wide)) for k in range(panel)]
        pivots = jnp.zeros((panel, wide), F32)
        for k in range(panel):
            pivot = columns[k][k : k + 1, :]
            factor = jnp.where(index > k, columns[k] * (1.0 / pivot), 0.0)
            pivots = jnp.where(index[:panel] == k, pivot, pivots)
            for m in range(k + 1, panel):
                columns[m] = columns[m] - factor * columns[m][k : k + 1, :]
            work = work - factor * work[k : k + 1, :]
        done.append(work[:panel, RANK:] * lax.rsqrt(pivots)[:, RANK:])
        work = work[panel:]
    return jnp.concatenate(done, axis=0)


def rows_of(coefficient_of, x_ref, x_last_ref):
    span = lambda i: pl.ds(i * FOLD_D, FOLD_D)
    groups = [jnp.zeros((GROUP, RANK), F32) for _ in range(ROWS // GROUP)]
    last = jnp.zeros((EXPERTS, RANK), F32)
    for i in range(SLOTS):
        coefficient = coefficient_of(i)
        for b in range(ROWS // GROUP):
            groups[b] = groups[b] + dot(x_ref[b * GROUP : (b + 1) * GROUP, span(i)], coefficient, (1, 1))
        last = last + dot(x_last_ref[:, span(i)], coefficient, (1, 1))
    main = jnp.concatenate([jnp.transpose(group) for group in groups], axis=1)
    return main.astype(BF16), jnp.transpose(last).astype(BF16)


def half_round(rows_main, rows_last, grads, grads_last):
    sketch = (dot(rows_main, grads, (1, 0)) + dot(rows_last, grads_last, (1, 0))).astype(BF16)
    gram = dot(sketch, sketch, (1, 1)) / FF
    main, last = dot(sketch, grads, (1, 1)), dot(sketch, grads_last, (1, 1))
    inverse = inverse_factor(gram)
    main, last = dot(inverse, main, (1, 0), HIGHEST), dot(inverse, last, (1, 0), HIGHEST)
    return sketch, inverse, main.astype(BF16), last.astype(BF16)


def rounds_kernel(data, place_ref, packed_ref, sketch_ref, *refs):
    outs, (x_last_ref, grads_last_ref, fold_ref, basis_ref) = refs[:data], refs[data:]
    span = lambda i: pl.ds(i * FOLD_D, FOLD_D)
    x_ref = packed_ref.at[:, pl.ds(0, D)]

    unfold(packed_ref, D, FOLD_D, x_last_ref, fold_ref)
    main, last = rows_of(lambda i: sketch_ref[:, span(i)], x_ref, x_last_ref)
    unfold(packed_ref, X_WIDTH + FF, FOLD_FF, grads_last_ref, fold_ref)
    grads, grads_last = packed_ref[:, X_WIDTH : X_WIDTH + FF], grads_last_ref[...]
    sketch, inverse, main, last = half_round(main, last, grads, grads_last)
    partial = lambda i: (dot(main, x_ref[:, span(i)], (1, 0)) + dot(last, x_last_ref[:, span(i)], (1, 0))) * SCALE
    for _ in range(POWER):
        main, last = rows_of(lambda i: partial(i).astype(BF16), x_ref, x_last_ref)
        sketch, inverse, main, last = half_round(main, last, grads, grads_last)
    basis = dot(inverse, sketch.astype(F32), (1, 0), HIGHEST).astype(BF16)
    basis_ref[...] = basis
    width, share = D // data, FF // data
    for k in range(data):
        g = lax.rem(place_ref[0] + k, data)
        outs[k][:, width:] = basis_ref[:, pl.ds(pl.multiple_of(g * share, share), share)]
        cols = pl.ds(pl.multiple_of(g * width, width), width)
        adapter = (dot(main, x_ref[:, cols], (1, 0)) + dot(last, x_last_ref[:, cols], (1, 0))) * SCALE
        outs[k][:, :width] = adapter.astype(BF16)


def rounds(place, packed, sketch_matrix, data):
    scalars, vmem = pl.BlockSpec(memory_space=pltpu.SMEM), pl.BlockSpec(memory_space=pltpu.VMEM)
    return pl.pallas_call(
        functools.partial(rounds_kernel, data),
        in_specs=[scalars, vmem, vmem],
        out_specs=(vmem,) * data,
        out_shape=(jax.ShapeDtypeStruct((RANK, (D + FF) // data), BF16),) * data,
        scratch_shapes=[
            pltpu.VMEM((EXPERTS, D), BF16),
            pltpu.VMEM((EXPERTS, FF), BF16),
            pltpu.VMEM((FOLD_D // 128, ROWS, 128), F32),
            pltpu.VMEM((RANK, FF), BF16),
        ],
        compiler_params=pltpu.CompilerParams(vmem_limit_bytes=ROUNDS_VMEM),
        cost_estimate=pl.CostEstimate(flops=40_000_000_000, bytes_accessed=24_000_000, transcendentals=0),
        name="rounds",
    )(place, packed, sketch_matrix)


def gather_kernel(data, place_ref, *refs):
    parts, (basis_ref, adapter_ref) = refs[:data], refs[data:]
    width = D // data
    for k in range(data):
        source = lax.rem(place_ref[0] - k + data, data)
        basis_ref[source] = parts[k][:, width:]
        adapter_ref[source] = parts[k][:, :width].astype(F32)


def gather(place, parts):
    data = len(parts)
    scalars, vmem = pl.BlockSpec(memory_space=pltpu.SMEM), pl.BlockSpec(memory_space=pltpu.VMEM)
    return pl.pallas_call(
        functools.partial(gather_kernel, data),
        in_specs=[scalars] + [vmem] * data,
        out_specs=(vmem, vmem),
        out_shape=(
            jax.ShapeDtypeStruct((data, RANK, FF // data), BF16),
            jax.ShapeDtypeStruct((data, RANK, D // data), F32),
        ),
        compiler_params=pltpu.CompilerParams(vmem_limit_bytes=16 * 1024 * 1024),
        cost_estimate=pl.CostEstimate(flops=0, bytes_accessed=3_000_000, transcendentals=0),
        name="gather",
    )(place, *parts)


def shards(tokens, cotangents, routing, sketch_matrix):
    per_group = EXPERTS // lax.axis_size("expert")
    data = lax.axis_size("dp")
    packed = pack(routing.T, tokens, cotangents.reshape(TOK_DEV * TOP, FF), per_group)
    packed = lax.all_to_all(
        packed.reshape(EXPERTS, SLOTS, WIDTH), ("dp", "expert"), split_axis=0, concat_axis=0, tiled=True
    ).reshape(ROWS, WIDTH)
    packed = pltpu.with_memory_space_constraint(packed, pltpu.VMEM)
    sketch_matrix = pltpu.with_memory_space_constraint(sketch_matrix, pltpu.VMEM)
    place = lax.axis_index("dp").reshape(1)
    parts = list(rounds(place, packed, sketch_matrix, data))
    for k in range(1, data):
        parts[k] = lax.ppermute(parts[k], "dp", [(i, (i + k) % data) for i in range(data)])
    return gather(place, parts)


def solution(mesh):
    in_specs = (
        P(("dp", "expert"), None),
        P(("dp", "expert"), None, None),
        P(("dp", "expert"), None),
        P(),
    )
    out_specs = (P("expert", None, "dp"), P("expert", None, "dp"))
    return jax.shard_map(shards, mesh=mesh, in_specs=in_specs, out_specs=out_specs, check_vma=False)
```

```python
import functools
import math

import jax
import jax.numpy as jnp
from jax import lax
from jax.experimental import pallas as pl
from jax.experimental.pallas import tpu as pltpu
from jax.sharding import PartitionSpec as P

D = 7168
FF = 2048
RANK = 64
TOP = 8
POWER = 2
TOK_DEV = 128
EXPERTS = 128
ROUTED = 1024
SLOTS = 8
ROWS = EXPERTS * SLOTS
FOLD_D = D // SLOTS
FOLD_FF = FF // SLOTS
X_WIDTH = D + FOLD_D
WIDTH = X_WIDTH + FF + FOLD_FF
G_CHUNK = 512
X_CHUNK = 2 * FOLD_D
GROUP = 256
RIDGE_SHIFT = 0.0001
SCALE = 1.0 / math.sqrt(FF * ROUTED)
VMEM = 56 * 1024 * 1024
ROUNDS_VMEM = 36 * 1024 * 1024
F32 = jnp.float32
BF16 = jnp.bfloat16
HIGHEST = lax.Precision.HIGHEST


def dot(a, b, contract, precision=None):
    return lax.dot_general(
        a, b, ((contract[:1], contract[1:]), ((), ())), precision=precision, preferred_element_type=F32
    )


def iota(shape, axis):
    return lax.broadcasted_iota(jnp.int32, shape, axis)


def ones_where(mask):
    return jnp.where(mask, 1.0, 0.0).astype(F32).astype(BF16)


def fold(rows, r, fold_ref):
    for h in range(rows.shape[1] // 128):
        fold_ref[h, pl.ds(r, EXPERTS, stride=SLOTS), :] = rows[:, h * 128 : (h + 1) * 128]


def unfold(packed_ref, start, width, rows_ref, fold_ref):
    for h in range(width // 128):
        fold_ref[h] = packed_ref[:, start + h * 128 : start + (h + 1) * 128].astype(F32)
    for r in range(SLOTS):
        for h in range(width // 128):
            c = r * width + h * 128
            rows_ref[:, c : c + 128] = fold_ref[h, pl.ds(r, EXPERTS, stride=SLOTS), :].astype(BF16)


def pack_kernel(per_group, routing_ref, tok_hbm, cot_hbm, out_hbm, tok_ref, cot_ref, out_ref, fold_ref, in_sems, out_sems):
    parts = [pl.ds(c, X_CHUNK) for c in range(0, D, X_CHUNK)]
    tok_copies = [
        pltpu.make_async_copy(tok_hbm.at[:, part], tok_ref.at[:, part], in_sems.at[r]) for r, part in enumerate(parts)
    ]
    for copy in tok_copies:
        copy.start()
    cot_copy = pltpu.make_async_copy(cot_hbm, cot_ref, in_sems.at[len(parts)])
    cot_copy.start()
    sent = []

    def send(start, width):
        span = pl.ds(start, width)
        copy = pltpu.make_async_copy(out_ref.at[:, span], out_hbm.at[:, span], out_sems.at[len(sent)])
        copy.start()
        sent.append(copy)

    expert = routing_ref[...]
    owner = (expert % per_group) * (EXPERTS // per_group) + expert // per_group
    square = (EXPERTS, TOK_DEV)
    device = iota(square, 0)
    named = jnp.zeros(square, F32)
    for k in range(TOP):
        named = named + jnp.where(owner[k : k + 1, :] == device, 1.0, 0.0)
    earlier = ones_where(iota(square, 0) < iota(square, 1))
    slot = jnp.where(named > 0.0, dot(named.astype(BF16), earlier, (1, 0)), -1.0)
    spread = ones_where(iota((ROWS, EXPERTS), 0) // SLOTS == iota((ROWS, EXPERTS), 1))
    row_slot = dot(spread, slot.astype(BF16), (1, 0))
    sel = ones_where(row_slot == (iota((ROWS, TOK_DEV), 0) % SLOTS).astype(F32))
    sel_last = ones_where(slot == float(SLOTS))
    for r, part in enumerate(parts):
        tok_copies[r].wait()
        out_ref[:, part] = dot(sel, tok_ref[:, part], (1, 0)).astype(BF16)
        send(r * X_CHUNK, X_CHUNK)
        rows = dot(sel_last, tok_ref[:, part], (1, 0))
        for q in range(X_CHUNK // FOLD_D):
            fold(rows[:, q * FOLD_D : (q + 1) * FOLD_D], r * (X_CHUNK // FOLD_D) + q, fold_ref)
    for h in range(FOLD_D // 128):
        out_ref[:, D + h * 128 : D + (h + 1) * 128] = fold_ref[h].astype(BF16)
    send(D, FOLD_D)

    pairs = (TOK_DEV, TOK_DEV * TOP)
    token_of = ones_where(iota(pairs, 1) // TOP == iota(pairs, 0))
    choices = dot(owner.astype(F32).astype(BF16), token_of, (1, 0))
    place = iota(choices.shape, 1) % TOP == iota(choices.shape, 0)
    flat = jnp.sum(jnp.where(place, choices, 0.0), axis=0, keepdims=True)
    row_owner = (iota((ROWS, 1), 0) // SLOTS).astype(F32)
    sel_pair = ones_where((dot(sel, token_of, (1, 0)) > 0.5) & (row_owner == flat))
    last_owner = iota((EXPERTS, 1), 0).astype(F32)
    last_pair = ones_where((dot(sel_last, token_of, (1, 0)) > 0.5) & (last_owner == flat))
    cot_copy.wait()
    for c in range(0, FF, G_CHUNK):
        out_ref[:, X_WIDTH + c : X_WIDTH + c + G_CHUNK] = dot(sel_pair, cot_ref[:, c : c + G_CHUNK], (1, 0)).astype(BF16)
        send(X_WIDTH + c, G_CHUNK)
        rows = dot(last_pair, cot_ref[:, c : c + G_CHUNK], (1, 0))
        for r in range(c // FOLD_FF, (c + G_CHUNK) // FOLD_FF):
            fold(rows[:, r * FOLD_FF - c : (r + 1) * FOLD_FF - c], r, fold_ref)
    for h in range(FOLD_FF // 128):
        start = X_WIDTH + FF + h * 128
        out_ref[:, start : start + 128] = fold_ref[h].astype(BF16)
    send(X_WIDTH + FF, FOLD_FF)
    for copy in sent:
        copy.wait()


def pack(routing_t, tokens, cot, per_group):
    anywhere, vmem = pl.BlockSpec(memory_space=pl.ANY), pl.BlockSpec(memory_space=pltpu.VMEM)
    return pl.pallas_call(
        functools.partial(pack_kernel, per_group),
        in_specs=[vmem, anywhere, anywhere],
        out_specs=anywhere,
        out_shape=jax.ShapeDtypeStruct((ROWS, WIDTH), BF16),
        scratch_shapes=[
            pltpu.VMEM((TOK_DEV, D), BF16),
            pltpu.VMEM((TOK_DEV * TOP, FF), BF16),
            pltpu.VMEM((ROWS, WIDTH), BF16),
            pltpu.VMEM((FOLD_D // 128, ROWS, 128), F32),
            pltpu.SemaphoreType.DMA((D // X_CHUNK + 1,)),
            pltpu.SemaphoreType.DMA((D // X_CHUNK + FF // G_CHUNK + 2,)),
        ],
        compiler_params=pltpu.CompilerParams(vmem_limit_bytes=VMEM),
        cost_estimate=pl.CostEstimate(flops=8_000_000_000, bytes_accessed=28_000_000, transcendentals=0),
        name="pack",
    )(routing_t, tokens, cot)


def inverse_factor(gram):
    panel, wide = 16, 2 * RANK
    rows, cols = iota((RANK, wide), 0), iota((RANK, wide), 1)
    diagonal = jnp.where(rows == cols, jnp.concatenate([gram, gram], axis=1), 0.0)
    mean = jnp.sum(jnp.sum(diagonal, axis=1, keepdims=True), axis=0, keepdims=True) / RANK
    work = jnp.concatenate([gram, jnp.zeros((RANK, RANK), F32)], axis=1)
    work = work + jnp.where(cols == rows + RANK, 1.0, 0.0) + jnp.where(rows == cols, RIDGE_SHIFT * mean, 0.0)
    done = []
    for j in range(0, RANK, panel):
        height = RANK - j
        index = iota((height, wide), 0)
        columns = [jnp.broadcast_to(work[:, j + k : j + k + 1], (height, wide)) for k in range(panel)]
        pivots = jnp.zeros((panel, wide), F32)
        for k in range(panel):
            pivot = columns[k][k : k + 1, :]
            factor = jnp.where(index > k, columns[k] * (1.0 / pivot), 0.0)
            pivots = jnp.where(index[:panel] == k, pivot, pivots)
            for m in range(k + 1, panel):
                columns[m] = columns[m] - factor * columns[m][k : k + 1, :]
            work = work - factor * work[k : k + 1, :]
        done.append(work[:panel, RANK:] * lax.rsqrt(pivots)[:, RANK:])
        work = work[panel:]
    return jnp.concatenate(done, axis=0)


def rows_of(coefficient_of, x_ref, x_last_ref):
    span = lambda i: pl.ds(i * FOLD_D, FOLD_D)
    groups = [jnp.zeros((GROUP, RANK), F32) for _ in range(ROWS // GROUP)]
    last = jnp.zeros((EXPERTS, RANK), F32)
    for i in range(SLOTS):
        coefficient = coefficient_of(i)
        for b in range(ROWS // GROUP):
            groups[b] = groups[b] + dot(x_ref[b * GROUP : (b + 1) * GROUP, span(i)], coefficient, (1, 1))
        last = last + dot(x_last_ref[:, span(i)], coefficient, (1, 1))
    main = jnp.concatenate([jnp.transpose(group) for group in groups], axis=1)
    return main.astype(BF16), jnp.transpose(last).astype(BF16)


def half_round(rows_main, rows_last, grads, grads_last):
    sketch = (dot(rows_main, grads, (1, 0)) + dot(rows_last, grads_last, (1, 0))).astype(BF16)
    gram = dot(sketch, sketch, (1, 1)) / FF
    main, last = dot(sketch, grads, (1, 1)), dot(sketch, grads_last, (1, 1))
    inverse = inverse_factor(gram)
    main, last = dot(inverse, main, (1, 0), HIGHEST), dot(inverse, last, (1, 0), HIGHEST)
    return sketch, inverse, main.astype(BF16), last.astype(BF16)


def rounds_kernel(data, packed_ref, sketch_hbm, *refs):
    outs, (x_last_ref, grads_last_ref, fold_ref, basis_ref, sketch_ref, sem) = refs[:data], refs[data:]
    span = lambda i: pl.ds(i * FOLD_D, FOLD_D)
    x_ref = packed_ref.at[:, pl.ds(0, D)]
    copy = pltpu.make_async_copy(sketch_hbm, sketch_ref, sem)
    copy.start()

    unfold(packed_ref, D, FOLD_D, x_last_ref, fold_ref)
    unfold(packed_ref, X_WIDTH + FF, FOLD_FF, grads_last_ref, fold_ref)
    copy.wait()
    main, last = rows_of(lambda i: sketch_ref[:, span(i)], x_ref, x_last_ref)
    grads, grads_last = packed_ref[:, X_WIDTH : X_WIDTH + FF], grads_last_ref[...]
    sketch, inverse, main, last = half_round(main, last, grads, grads_last)
    partial = lambda i: (dot(main, x_ref[:, span(i)], (1, 0)) + dot(last, x_last_ref[:, span(i)], (1, 0))) * SCALE
    for _ in range(POWER):
        main, last = rows_of(lambda i: partial(i).astype(BF16), x_ref, x_last_ref)
        sketch, inverse, main, last = half_round(main, last, grads, grads_last)
    basis = dot(inverse, sketch.astype(F32), (1, 0), HIGHEST).astype(BF16)
    basis_ref[...] = basis
    width, share = D // data, FF // data
    place = lax.axis_index("dp")
    for k in range(data):
        g = lax.rem(place + k, data)
        outs[k][:, width:] = basis_ref[:, pl.ds(pl.multiple_of(g * share, share), share)]
        cols = pl.ds(pl.multiple_of(g * width, width), width)
        adapter = (dot(main, x_ref[:, cols], (1, 0)) + dot(last, x_last_ref[:, cols], (1, 0))) * SCALE
        outs[k][:, :width] = adapter.astype(BF16)


def rounds(packed, sketch_matrix, data):
    anywhere, vmem = pl.BlockSpec(memory_space=pl.ANY), pl.BlockSpec(memory_space=pltpu.VMEM)
    return pl.pallas_call(
        functools.partial(rounds_kernel, data),
        in_specs=[vmem, anywhere],
        out_specs=(vmem,) * data,
        out_shape=(jax.ShapeDtypeStruct((RANK, (D + FF) // data), BF16),) * data,
        scratch_shapes=[
            pltpu.VMEM((EXPERTS, D), BF16),
            pltpu.VMEM((EXPERTS, FF), BF16),
            pltpu.VMEM((FOLD_D // 128, ROWS, 128), F32),
            pltpu.VMEM((RANK, FF), BF16),
            pltpu.VMEM((RANK, D), BF16),
            pltpu.SemaphoreType.DMA,
        ],
        compiler_params=pltpu.CompilerParams(vmem_limit_bytes=ROUNDS_VMEM),
        cost_estimate=pl.CostEstimate(flops=40_000_000_000, bytes_accessed=24_000_000, transcendentals=0),
        name="rounds",
    )(packed, sketch_matrix)


def gather_kernel(data, *refs):
    place = lax.axis_index("dp")
    parts, (basis_ref, adapter_ref) = refs[:data], refs[data:]
    width = D // data
    for k in range(data):
        source = lax.rem(place - k + data, data)
        basis_ref[source] = parts[k][:, width:]
        adapter_ref[source] = parts[k][:, :width].astype(F32)


def gather(parts):
    data = len(parts)
    vmem = pl.BlockSpec(memory_space=pltpu.VMEM)
    return pl.pallas_call(
        functools.partial(gather_kernel, data),
        in_specs=[vmem] * data,
        out_specs=(vmem, vmem),
        out_shape=(
            jax.ShapeDtypeStruct((data, RANK, FF // data), BF16),
            jax.ShapeDtypeStruct((data, RANK, D // data), F32),
        ),
        compiler_params=pltpu.CompilerParams(vmem_limit_bytes=16 * 1024 * 1024),
        cost_estimate=pl.CostEstimate(flops=0, bytes_accessed=3_000_000, transcendentals=0),
        name="gather",
    )(*parts)


def shards(tokens, cotangents, routing, sketch_matrix):
    per_group = EXPERTS // lax.axis_size("expert")
    data = lax.axis_size("dp")
    packed = pack(routing.T, tokens, cotangents.reshape(TOK_DEV * TOP, FF), per_group)
    packed = lax.all_to_all(
        packed.reshape(EXPERTS, SLOTS, WIDTH), ("dp", "expert"), split_axis=0, concat_axis=0, tiled=True
    ).reshape(ROWS, WIDTH)
    packed = pltpu.with_memory_space_constraint(packed, pltpu.VMEM)
    parts = list(rounds(packed, sketch_matrix, data))
    for k in range(1, data):
        parts[k] = lax.ppermute(parts[k], "dp", [(i, (i + k) % data) for i in range(data)])
    return gather(parts)


def solution(mesh):
    in_specs = (
        P(("dp", "expert"), None),
        P(("dp", "expert"), None, None),
        P(("dp", "expert"), None),
        P(),
    )
    out_specs = (P("expert", None, "dp"), P("expert", None, "dp"))
    return jax.shard_map(shards, mesh=mesh, in_specs=in_specs, out_specs=out_specs, check_vma=False)
```

```python
import functools
import math

import jax
import jax.numpy as jnp
from jax import lax
from jax.experimental import pallas as pl
from jax.experimental.pallas import tpu as pltpu
from jax.sharding import PartitionSpec as P

D = 7168
FF = 2048
RANK = 64
TOP = 8
POWER = 2
TOK_DEV = 128
EXPERTS = 128
ROUTED = 1024
SLOTS = 8
ROWS = EXPERTS * SLOTS
FOLD_D = D // SLOTS
FOLD_FF = FF // SLOTS
X_WIDTH = D + FOLD_D
WIDTH = X_WIDTH + FF + FOLD_FF
G_CHUNK = 512
X_CHUNK = 2 * FOLD_D
GROUP = 256
RIDGE_SHIFT = 0.0001
SCALE = 1.0 / math.sqrt(FF * ROUTED)
VMEM = 56 * 1024 * 1024
ROUNDS_VMEM = 36 * 1024 * 1024
F32 = jnp.float32
BF16 = jnp.bfloat16
HIGHEST = lax.Precision.HIGHEST


def dot(a, b, contract, precision=None):
    return lax.dot_general(
        a, b, ((contract[:1], contract[1:]), ((), ())), precision=precision, preferred_element_type=F32
    )


def iota(shape, axis):
    return lax.broadcasted_iota(jnp.int32, shape, axis)


def ones_where(mask):
    return jnp.where(mask, 1.0, 0.0).astype(F32).astype(BF16)


def fold(rows, r, fold_ref):
    for h in range(rows.shape[1] // 128):
        fold_ref[h, pl.ds(r, EXPERTS, stride=SLOTS), :] = rows[:, h * 128 : (h + 1) * 128]


def unfold(packed_ref, start, width, rows_ref, fold_ref):
    for h in range(width // 128):
        fold_ref[h] = packed_ref[:, start + h * 128 : start + (h + 1) * 128].astype(F32)
    for r in range(SLOTS):
        for h in range(width // 128):
            c = r * width + h * 128
            rows_ref[:, c : c + 128] = fold_ref[h, pl.ds(r, EXPERTS, stride=SLOTS), :].astype(BF16)


def pack_kernel(per_group, routing_ref, tok_hbm, cot_hbm, out_hbm, tok_ref, cot_ref, out_ref, fold_ref, in_sems, out_sems):
    parts = [pl.ds(c, X_CHUNK) for c in range(0, D, X_CHUNK)]
    tok_copies = [
        pltpu.make_async_copy(tok_hbm.at[:, part], tok_ref.at[:, part], in_sems.at[r]) for r, part in enumerate(parts)
    ]
    for copy in tok_copies:
        copy.start()
    cot_copy = pltpu.make_async_copy(cot_hbm, cot_ref, in_sems.at[len(parts)])
    cot_copy.start()
    sent = []

    def send(start, width):
        span = pl.ds(start, width)
        copy = pltpu.make_async_copy(out_ref.at[:, span], out_hbm.at[:, span], out_sems.at[len(sent)])
        copy.start()
        sent.append(copy)

    expert = routing_ref[...]
    owner = (expert % per_group) * (EXPERTS // per_group) + expert // per_group
    square = (EXPERTS, TOK_DEV)
    device = iota(square, 0)
    named = jnp.zeros(square, F32)
    for k in range(TOP):
        named = named + jnp.where(owner[k : k + 1, :] == device, 1.0, 0.0)
    earlier = ones_where(iota(square, 0) < iota(square, 1))
    slot = jnp.where(named > 0.0, dot(named.astype(BF16), earlier, (1, 0)), -1.0)
    spread = ones_where(iota((ROWS, EXPERTS), 0) // SLOTS == iota((ROWS, EXPERTS), 1))
    row_slot = dot(spread, slot.astype(BF16), (1, 0))
    sel = ones_where(row_slot == (iota((ROWS, TOK_DEV), 0) % SLOTS).astype(F32))
    sel_last = ones_where(slot == float(SLOTS))
    for r, part in enumerate(parts):
        tok_copies[r].wait()
        out_ref[:, part] = dot(sel, tok_ref[:, part], (1, 0)).astype(BF16)
        send(r * X_CHUNK, X_CHUNK)
        rows = dot(sel_last, tok_ref[:, part], (1, 0))
        for q in range(X_CHUNK // FOLD_D):
            fold(rows[:, q * FOLD_D : (q + 1) * FOLD_D], r * (X_CHUNK // FOLD_D) + q, fold_ref)
    for h in range(FOLD_D // 128):
        out_ref[:, D + h * 128 : D + (h + 1) * 128] = fold_ref[h].astype(BF16)
    send(D, FOLD_D)

    pairs = (TOK_DEV, TOK_DEV * TOP)
    token_of = ones_where(iota(pairs, 1) // TOP == iota(pairs, 0))
    choices = dot(owner.astype(F32).astype(BF16), token_of, (1, 0))
    place = iota(choices.shape, 1) % TOP == iota(choices.shape, 0)
    flat = jnp.sum(jnp.where(place, choices, 0.0), axis=0, keepdims=True)
    row_owner = (iota((ROWS, 1), 0) // SLOTS).astype(F32)
    sel_pair = ones_where((dot(sel, token_of, (1, 0)) > 0.5) & (row_owner == flat))
    last_owner = iota((EXPERTS, 1), 0).astype(F32)
    last_pair = ones_where((dot(sel_last, token_of, (1, 0)) > 0.5) & (last_owner == flat))
    cot_copy.wait()
    for c in range(0, FF, G_CHUNK):
        out_ref[:, X_WIDTH + c : X_WIDTH + c + G_CHUNK] = dot(sel_pair, cot_ref[:, c : c + G_CHUNK], (1, 0)).astype(BF16)
        send(X_WIDTH + c, G_CHUNK)
        rows = dot(last_pair, cot_ref[:, c : c + G_CHUNK], (1, 0))
        for r in range(c // FOLD_FF, (c + G_CHUNK) // FOLD_FF):
            fold(rows[:, r * FOLD_FF - c : (r + 1) * FOLD_FF - c], r, fold_ref)
    for h in range(FOLD_FF // 128):
        start = X_WIDTH + FF + h * 128
        out_ref[:, start : start + 128] = fold_ref[h].astype(BF16)
    send(X_WIDTH + FF, FOLD_FF)
    for copy in sent:
        copy.wait()


def pack(routing_t, tokens, cot, per_group):
    anywhere, vmem = pl.BlockSpec(memory_space=pl.ANY), pl.BlockSpec(memory_space=pltpu.VMEM)
    return pl.pallas_call(
        functools.partial(pack_kernel, per_group),
        in_specs=[vmem, anywhere, anywhere],
        out_specs=anywhere,
        out_shape=jax.ShapeDtypeStruct((ROWS, WIDTH), BF16),
        scratch_shapes=[
            pltpu.VMEM((TOK_DEV, D), BF16),
            pltpu.VMEM((TOK_DEV * TOP, FF), BF16),
            pltpu.VMEM((ROWS, WIDTH), BF16),
            pltpu.VMEM((FOLD_D // 128, ROWS, 128), F32),
            pltpu.SemaphoreType.DMA((D // X_CHUNK + 1,)),
            pltpu.SemaphoreType.DMA((D // X_CHUNK + FF // G_CHUNK + 2,)),
        ],
        compiler_params=pltpu.CompilerParams(vmem_limit_bytes=VMEM),
        cost_estimate=pl.CostEstimate(flops=8_000_000_000, bytes_accessed=28_000_000, transcendentals=0),
        name="pack",
    )(routing_t, tokens, cot)


def inverse_factor(gram):
    panel, wide = 16, 2 * RANK
    rows, cols = iota((RANK, wide), 0), iota((RANK, wide), 1)
    diagonal = jnp.where(rows == cols, jnp.concatenate([gram, gram], axis=1), 0.0)
    mean = jnp.sum(jnp.sum(diagonal, axis=1, keepdims=True), axis=0, keepdims=True) / RANK
    work = jnp.concatenate([gram, jnp.zeros((RANK, RANK), F32)], axis=1)
    work = work + jnp.where(cols == rows + RANK, 1.0, 0.0) + jnp.where(rows == cols, RIDGE_SHIFT * mean, 0.0)
    done = []
    for j in range(0, RANK, panel):
        height = RANK - j
        index = iota((height, wide), 0)
        columns = [jnp.broadcast_to(work[:, j + k : j + k + 1], (height, wide)) for k in range(panel)]
        pivots = jnp.zeros((panel, wide), F32)
        for k in range(panel):
            pivot = columns[k][k : k + 1, :]
            factor = jnp.where(index > k, columns[k] * (1.0 / pivot), 0.0)
            pivots = jnp.where(index[:panel] == k, pivot, pivots)
            for m in range(k + 1, panel):
                columns[m] = columns[m] - factor * columns[m][k : k + 1, :]
            work = work - factor * work[k : k + 1, :]
        done.append(work[:panel, RANK:] * lax.rsqrt(pivots)[:, RANK:])
        work = work[panel:]
    return jnp.concatenate(done, axis=0)


def rows_of(coefficient_of, x_ref, x_last_ref):
    span = lambda i: pl.ds(i * FOLD_D, FOLD_D)
    groups = [jnp.zeros((GROUP, RANK), F32) for _ in range(ROWS // GROUP)]
    last = jnp.zeros((EXPERTS, RANK), F32)
    for i in range(SLOTS):
        coefficient = coefficient_of(i)
        for b in range(ROWS // GROUP):
            groups[b] = groups[b] + dot(x_ref[b * GROUP : (b + 1) * GROUP, span(i)], coefficient, (1, 1))
        last = last + dot(x_last_ref[:, span(i)], coefficient, (1, 1))
    main = jnp.concatenate([jnp.transpose(group) for group in groups], axis=1)
    return main.astype(BF16), jnp.transpose(last).astype(BF16)


def half_round(rows_main, rows_last, grads, grads_last):
    sketch = (dot(rows_main, grads, (1, 0)) + dot(rows_last, grads_last, (1, 0))).astype(BF16)
    gram = dot(sketch, sketch, (1, 1)) / FF
    main, last = dot(sketch, grads, (1, 1)), dot(sketch, grads_last, (1, 1))
    inverse = inverse_factor(gram)
    main, last = dot(inverse, main, (1, 0), HIGHEST), dot(inverse, last, (1, 0), HIGHEST)
    return sketch, inverse, main.astype(BF16), last.astype(BF16)


def rounds_kernel(data, packed_ref, sketch_hbm, *refs):
    outs, (x_last_ref, grads_last_ref, fold_ref, basis_ref, sketch_ref, sem) = refs[:data], refs[data:]
    span = lambda i: pl.ds(i * FOLD_D, FOLD_D)
    x_ref = packed_ref.at[:, pl.ds(0, D)]
    copy = pltpu.make_async_copy(sketch_hbm, sketch_ref, sem)
    copy.start()

    unfold(packed_ref, D, FOLD_D, x_last_ref, fold_ref)
    unfold(packed_ref, X_WIDTH + FF, FOLD_FF, grads_last_ref, fold_ref)
    copy.wait()
    main, last = rows_of(lambda i: sketch_ref[:, span(i)], x_ref, x_last_ref)
    grads, grads_last = packed_ref[:, X_WIDTH : X_WIDTH + FF], grads_last_ref[...]
    sketch, inverse, main, last = half_round(main, last, grads, grads_last)
    partial = lambda i: (dot(main, x_ref[:, span(i)], (1, 0)) + dot(last, x_last_ref[:, span(i)], (1, 0))) * SCALE
    for _ in range(POWER):
        main, last = rows_of(lambda i: partial(i).astype(BF16), x_ref, x_last_ref)
        sketch, inverse, main, last = half_round(main, last, grads, grads_last)
    basis = dot(inverse, sketch.astype(F32), (1, 0), HIGHEST).astype(BF16)
    basis_ref[...] = basis
    width, share = D // data, FF // data
    place = lax.axis_index("dp")
    for k in range(data):
        g = lax.rem(place + k, data)
        outs[k][:, width:] = basis_ref[:, pl.ds(pl.multiple_of(g * share, share), share)]
        cols = pl.ds(pl.multiple_of(g * width, width), width)
        adapter = (dot(main, x_ref[:, cols], (1, 0)) + dot(last, x_last_ref[:, cols], (1, 0))) * SCALE
        outs[k][:, :width] = adapter.astype(BF16)


def rounds(packed, sketch_matrix, data):
    anywhere, vmem = pl.BlockSpec(memory_space=pl.ANY), pl.BlockSpec(memory_space=pltpu.VMEM)
    return pl.pallas_call(
        functools.partial(rounds_kernel, data),
        in_specs=[vmem, anywhere],
        out_specs=(vmem,) * data,
        out_shape=(pltpu.VMEM((RANK, (D + FF) // data), BF16),)
        + (jax.ShapeDtypeStruct((RANK, (D + FF) // data), BF16),) * (data - 1),
        scratch_shapes=[
            pltpu.VMEM((EXPERTS, D), BF16),
            pltpu.VMEM((EXPERTS, FF), BF16),
            pltpu.VMEM((FOLD_D // 128, ROWS, 128), F32),
            pltpu.VMEM((RANK, FF), BF16),
            pltpu.VMEM((RANK, D), BF16),
            pltpu.SemaphoreType.DMA,
        ],
        compiler_params=pltpu.CompilerParams(vmem_limit_bytes=ROUNDS_VMEM),
        cost_estimate=pl.CostEstimate(flops=40_000_000_000, bytes_accessed=24_000_000, transcendentals=0),
        name="rounds",
    )(packed, sketch_matrix)


def gather_kernel(data, *refs):
    place = lax.axis_index("dp")
    parts, (basis_ref, adapter_ref) = refs[:data], refs[data:]
    width = D // data
    for k in range(data):
        source = lax.rem(place - k + data, data)
        basis_ref[source] = parts[k][:, width:]
        adapter_ref[source] = parts[k][:, :width].astype(F32)


def gather(parts):
    data = len(parts)
    vmem = pl.BlockSpec(memory_space=pltpu.VMEM)
    return pl.pallas_call(
        functools.partial(gather_kernel, data),
        in_specs=[vmem] * data,
        out_specs=(vmem, vmem),
        out_shape=(
            jax.ShapeDtypeStruct((data, RANK, FF // data), BF16),
            jax.ShapeDtypeStruct((data, RANK, D // data), F32),
        ),
        compiler_params=pltpu.CompilerParams(vmem_limit_bytes=16 * 1024 * 1024),
        cost_estimate=pl.CostEstimate(flops=0, bytes_accessed=3_000_000, transcendentals=0),
        name="gather",
    )(*parts)


def shards(tokens, cotangents, routing, sketch_matrix):
    per_group = EXPERTS // lax.axis_size("expert")
    data = lax.axis_size("dp")
    packed = pack(routing.T, tokens, cotangents.reshape(TOK_DEV * TOP, FF), per_group)
    packed = lax.all_to_all(
        packed.reshape(EXPERTS, SLOTS, WIDTH), ("dp", "expert"), split_axis=0, concat_axis=0, tiled=True
    ).reshape(ROWS, WIDTH)
    packed = pltpu.with_memory_space_constraint(packed, pltpu.VMEM)
    parts = list(rounds(packed, sketch_matrix, data))
    for k in range(1, data):
        parts[k] = lax.ppermute(parts[k], "dp", [(i, (i + k) % data) for i in range(data)])
    return gather(parts)


def solution(mesh):
    in_specs = (
        P(("dp", "expert"), None),
        P(("dp", "expert"), None, None),
        P(("dp", "expert"), None),
        P(),
    )
    out_specs = (P("expert", None, "dp"), P("expert", None, "dp"))
    return jax.shard_map(shards, mesh=mesh, in_specs=in_specs, out_specs=out_specs, check_vma=False)
```

```python
import functools
import math

import jax
import jax.numpy as jnp
from jax import lax
from jax.experimental import pallas as pl
from jax.experimental.pallas import tpu as pltpu
from jax.sharding import PartitionSpec as P

D = 7168
FF = 2048
RANK = 64
TOP = 8
POWER = 2
TOK_DEV = 128
EXPERTS = 128
ROUTED = 1024
SLOTS = 8
ROWS = EXPERTS * SLOTS
FOLD_D = D // SLOTS
FOLD_FF = FF // SLOTS
X_WIDTH = D + FOLD_D
WIDTH = X_WIDTH + FF + FOLD_FF
G_CHUNK = 512
X_CHUNK = 2 * FOLD_D
GROUP = 256
RIDGE_SHIFT = 0.0001
SCALE = 1.0 / math.sqrt(FF * ROUTED)
VMEM = 56 * 1024 * 1024
ROUNDS_VMEM = 36 * 1024 * 1024
F32 = jnp.float32
BF16 = jnp.bfloat16
HIGHEST = lax.Precision.HIGHEST


def dot(a, b, contract, precision=None):
    return lax.dot_general(
        a, b, ((contract[:1], contract[1:]), ((), ())), precision=precision, preferred_element_type=F32
    )


def iota(shape, axis):
    return lax.broadcasted_iota(jnp.int32, shape, axis)


def ones_where(mask):
    return jnp.where(mask, 1.0, 0.0).astype(F32).astype(BF16)


def fold(rows, r, fold_ref):
    for h in range(rows.shape[1] // 128):
        fold_ref[h, pl.ds(r, EXPERTS, stride=SLOTS), :] = rows[:, h * 128 : (h + 1) * 128]


def unfold(packed_ref, start, width, rows_ref, fold_ref):
    for h in range(width // 128):
        fold_ref[h] = packed_ref[:, start + h * 128 : start + (h + 1) * 128].astype(F32)
    for r in range(SLOTS):
        for h in range(width // 128):
            c = r * width + h * 128
            rows_ref[:, c : c + 128] = fold_ref[h, pl.ds(r, EXPERTS, stride=SLOTS), :].astype(BF16)


def pack_kernel(per_group, routing_ref, tok_hbm, cot_hbm, out_hbm, tok_ref, cot_ref, out_ref, fold_ref, in_sems, out_sems):
    parts = [pl.ds(c, X_CHUNK) for c in range(0, D, X_CHUNK)]
    tok_copies = [
        pltpu.make_async_copy(tok_hbm.at[:, part], tok_ref.at[:, part], in_sems.at[r]) for r, part in enumerate(parts)
    ]
    for copy in tok_copies:
        copy.start()
    cot_copy = pltpu.make_async_copy(cot_hbm, cot_ref, in_sems.at[len(parts)])
    cot_copy.start()
    sent = []

    def send(start, width):
        span = pl.ds(start, width)
        copy = pltpu.make_async_copy(out_ref.at[:, span], out_hbm.at[:, span], out_sems.at[len(sent)])
        copy.start()
        sent.append(copy)

    expert = routing_ref[...]
    owner = (expert % per_group) * (EXPERTS // per_group) + expert // per_group
    square = (EXPERTS, TOK_DEV)
    device = iota(square, 0)
    named = jnp.zeros(square, F32)
    for k in range(TOP):
        named = named + jnp.where(owner[k : k + 1, :] == device, 1.0, 0.0)
    earlier = ones_where(iota(square, 0) < iota(square, 1))
    slot = jnp.where(named > 0.0, dot(named.astype(BF16), earlier, (1, 0)), -1.0)
    spread = ones_where(iota((ROWS, EXPERTS), 0) // SLOTS == iota((ROWS, EXPERTS), 1))
    row_slot = dot(spread, slot.astype(BF16), (1, 0))
    sel = ones_where(row_slot == (iota((ROWS, TOK_DEV), 0) % SLOTS).astype(F32))
    sel_last = ones_where(slot == float(SLOTS))
    for r, part in enumerate(parts):
        tok_copies[r].wait()
        out_ref[:, part] = dot(sel, tok_ref[:, part], (1, 0)).astype(BF16)
        send(r * X_CHUNK, X_CHUNK)
        rows = dot(sel_last, tok_ref[:, part], (1, 0))
        for q in range(X_CHUNK // FOLD_D):
            fold(rows[:, q * FOLD_D : (q + 1) * FOLD_D], r * (X_CHUNK // FOLD_D) + q, fold_ref)
    for h in range(FOLD_D // 128):
        out_ref[:, D + h * 128 : D + (h + 1) * 128] = fold_ref[h].astype(BF16)
    send(D, FOLD_D)

    pairs = (TOK_DEV, TOK_DEV * TOP)
    token_of = ones_where(iota(pairs, 1) // TOP == iota(pairs, 0))
    choices = dot(owner.astype(F32).astype(BF16), token_of, (1, 0))
    place = iota(choices.shape, 1) % TOP == iota(choices.shape, 0)
    flat = jnp.sum(jnp.where(place, choices, 0.0), axis=0, keepdims=True)
    row_owner = (iota((ROWS, 1), 0) // SLOTS).astype(F32)
    sel_pair = ones_where((dot(sel, token_of, (1, 0)) > 0.5) & (row_owner == flat))
    last_owner = iota((EXPERTS, 1), 0).astype(F32)
    last_pair = ones_where((dot(sel_last, token_of, (1, 0)) > 0.5) & (last_owner == flat))
    cot_copy.wait()
    for c in range(0, FF, G_CHUNK):
        out_ref[:, X_WIDTH + c : X_WIDTH + c + G_CHUNK] = dot(sel_pair, cot_ref[:, c : c + G_CHUNK], (1, 0)).astype(BF16)
        send(X_WIDTH + c, G_CHUNK)
        rows = dot(last_pair, cot_ref[:, c : c + G_CHUNK], (1, 0))
        for r in range(c // FOLD_FF, (c + G_CHUNK) // FOLD_FF):
            fold(rows[:, r * FOLD_FF - c : (r + 1) * FOLD_FF - c], r, fold_ref)
    for h in range(FOLD_FF // 128):
        start = X_WIDTH + FF + h * 128
        out_ref[:, start : start + 128] = fold_ref[h].astype(BF16)
    send(X_WIDTH + FF, FOLD_FF)
    for copy in sent:
        copy.wait()


def pack(routing_t, tokens, cot, per_group):
    anywhere, vmem = pl.BlockSpec(memory_space=pl.ANY), pl.BlockSpec(memory_space=pltpu.VMEM)
    return pl.pallas_call(
        functools.partial(pack_kernel, per_group),
        in_specs=[vmem, anywhere, anywhere],
        out_specs=anywhere,
        out_shape=jax.ShapeDtypeStruct((ROWS, WIDTH), BF16),
        scratch_shapes=[
            pltpu.VMEM((TOK_DEV, D), BF16),
            pltpu.VMEM((TOK_DEV * TOP, FF), BF16),
            pltpu.VMEM((ROWS, WIDTH), BF16),
            pltpu.VMEM((FOLD_D // 128, ROWS, 128), F32),
            pltpu.SemaphoreType.DMA((D // X_CHUNK + 1,)),
            pltpu.SemaphoreType.DMA((D // X_CHUNK + FF // G_CHUNK + 2,)),
        ],
        compiler_params=pltpu.CompilerParams(vmem_limit_bytes=VMEM),
        cost_estimate=pl.CostEstimate(flops=8_000_000_000, bytes_accessed=28_000_000, transcendentals=0),
        name="pack",
    )(routing_t, tokens, cot)


def inverse_factor(gram):
    panel, wide = 16, 2 * RANK
    rows, cols = iota((RANK, wide), 0), iota((RANK, wide), 1)
    diagonal = jnp.where(rows == cols, jnp.concatenate([gram, gram], axis=1), 0.0)
    mean = jnp.sum(jnp.sum(diagonal, axis=1, keepdims=True), axis=0, keepdims=True) / RANK
    work = jnp.concatenate([gram, jnp.zeros((RANK, RANK), F32)], axis=1)
    work = work + jnp.where(cols == rows + RANK, 1.0, 0.0) + jnp.where(rows == cols, RIDGE_SHIFT * mean, 0.0)
    done = []
    for j in range(0, RANK, panel):
        height = RANK - j
        index = iota((height, wide), 0)
        columns = [jnp.broadcast_to(work[:, j + k : j + k + 1], (height, wide)) for k in range(panel)]
        pivots = jnp.zeros((panel, wide), F32)
        for k in range(panel):
            pivot = columns[k][k : k + 1, :]
            factor = jnp.where(index > k, columns[k] * (1.0 / pivot), 0.0)
            pivots = jnp.where(index[:panel] == k, pivot, pivots)
            for m in range(k + 1, panel):
                columns[m] = columns[m] - factor * columns[m][k : k + 1, :]
            work = work - factor * work[k : k + 1, :]
        done.append(work[:panel, RANK:] * lax.rsqrt(pivots)[:, RANK:])
        work = work[panel:]
    return jnp.concatenate(done, axis=0)


def rows_of(coefficient_of, x_ref, x_last_ref):
    span = lambda i: pl.ds(i * FOLD_D, FOLD_D)
    groups = [jnp.zeros((GROUP, RANK), F32) for _ in range(ROWS // GROUP)]
    last = jnp.zeros((EXPERTS, RANK), F32)
    for i in range(SLOTS):
        coefficient = coefficient_of(i)
        for b in range(ROWS // GROUP):
            groups[b] = groups[b] + dot(x_ref[b * GROUP : (b + 1) * GROUP, span(i)], coefficient, (1, 1))
        last = last + dot(x_last_ref[:, span(i)], coefficient, (1, 1))
    main = jnp.concatenate([jnp.transpose(group) for group in groups], axis=1)
    return main.astype(BF16), jnp.transpose(last).astype(BF16)


def half_round(rows_main, rows_last, grads, grads_last):
    sketch = (dot(rows_main, grads, (1, 0)) + dot(rows_last, grads_last, (1, 0))).astype(BF16)
    gram = dot(sketch, sketch, (1, 1)) / FF
    main, last = dot(sketch, grads, (1, 1)), dot(sketch, grads_last, (1, 1))
    inverse = inverse_factor(gram)
    main, last = dot(inverse, main, (1, 0), HIGHEST), dot(inverse, last, (1, 0), HIGHEST)
    return sketch, inverse, main.astype(BF16), last.astype(BF16)


def rounds_kernel(data, packed_ref, sketch_hbm, *refs):
    outs, (x_last_ref, grads_last_ref, fold_ref, basis_ref, sketch_ref, sem) = refs[:data], refs[data:]
    span = lambda i: pl.ds(i * FOLD_D, FOLD_D)
    x_ref = packed_ref.at[:, pl.ds(0, D)]
    copy = pltpu.make_async_copy(sketch_hbm, sketch_ref, sem)
    copy.start()

    unfold(packed_ref, D, FOLD_D, x_last_ref, fold_ref)
    unfold(packed_ref, X_WIDTH + FF, FOLD_FF, grads_last_ref, fold_ref)
    copy.wait()
    main, last = rows_of(lambda i: sketch_ref[:, span(i)], x_ref, x_last_ref)
    grads, grads_last = packed_ref[:, X_WIDTH : X_WIDTH + FF], grads_last_ref[...]
    sketch, inverse, main, last = half_round(main, last, grads, grads_last)
    partial = lambda i: (dot(main, x_ref[:, span(i)], (1, 0)) + dot(last, x_last_ref[:, span(i)], (1, 0))) * SCALE
    for _ in range(POWER):
        main, last = rows_of(lambda i: partial(i).astype(BF16), x_ref, x_last_ref)
        sketch, inverse, main, last = half_round(main, last, grads, grads_last)
    basis = dot(inverse, sketch.astype(F32), (1, 0), HIGHEST).astype(BF16)
    basis_ref[...] = basis
    width, share = D // data, FF // data
    place = lax.axis_index("dp")
    for k in range(data):
        g = lax.rem(place + k, data)
        outs[k][:, width:] = basis_ref[:, pl.ds(pl.multiple_of(g * share, share), share)]
        cols = pl.ds(pl.multiple_of(g * width, width), width)
        adapter = (dot(main, x_ref[:, cols], (1, 0)) + dot(last, x_last_ref[:, cols], (1, 0))) * SCALE
        outs[k][:, :width] = adapter.astype(BF16)


def rounds(packed, sketch_matrix, data):
    anywhere, vmem = pl.BlockSpec(memory_space=pl.ANY), pl.BlockSpec(memory_space=pltpu.VMEM)
    return pl.pallas_call(
        functools.partial(rounds_kernel, data),
        in_specs=[vmem, anywhere],
        out_specs=(vmem,) * data,
        out_shape=(pltpu.VMEM((RANK, (D + FF) // data), BF16),)
        + (jax.ShapeDtypeStruct((RANK, (D + FF) // data), BF16),) * (data - 1),
        scratch_shapes=[
            pltpu.VMEM((EXPERTS, D), BF16),
            pltpu.VMEM((EXPERTS, FF), BF16),
            pltpu.VMEM((FOLD_D // 128, ROWS, 128), F32),
            pltpu.VMEM((RANK, FF), BF16),
            pltpu.VMEM((RANK, D), BF16),
            pltpu.SemaphoreType.DMA,
        ],
        compiler_params=pltpu.CompilerParams(vmem_limit_bytes=ROUNDS_VMEM),
        cost_estimate=pl.CostEstimate(flops=40_000_000_000, bytes_accessed=24_000_000, transcendentals=0),
        name="rounds",
    )(packed, sketch_matrix)


def gather_kernel(data, *refs):
    place = lax.axis_index("dp")
    parts, (basis_ref, adapter_ref) = refs[:data], refs[data:]
    width = D // data
    for k in range(data):
        source = lax.rem(place - k + data, data)
        basis_ref[source] = parts[k][:, width:]
        adapter_ref[source] = parts[k][:, :width].astype(F32)


def gather(parts):
    data = len(parts)
    vmem = pl.BlockSpec(memory_space=pltpu.VMEM)
    return pl.pallas_call(
        functools.partial(gather_kernel, data),
        in_specs=[vmem] * data,
        out_specs=(vmem, vmem),
        out_shape=(
            jax.ShapeDtypeStruct((data, RANK, FF // data), BF16),
            jax.ShapeDtypeStruct((data, RANK, D // data), F32),
        ),
        compiler_params=pltpu.CompilerParams(vmem_limit_bytes=16 * 1024 * 1024),
        cost_estimate=pl.CostEstimate(flops=0, bytes_accessed=3_000_000, transcendentals=0),
        name="gather",
    )(*parts)


def shards(tokens, cotangents, routing, sketch_matrix):
    per_group = EXPERTS // lax.axis_size("expert")
    data = lax.axis_size("dp")
    packed = pack(routing.T, tokens, cotangents.reshape(TOK_DEV * TOP, FF), per_group)
    packed = lax.all_to_all(
        packed.reshape(EXPERTS, SLOTS, WIDTH), ("dp", "expert"), split_axis=0, concat_axis=0, tiled=True
    ).reshape(ROWS, WIDTH)
    packed = pltpu.with_memory_space_constraint(packed, pltpu.VMEM)
    parts = list(rounds(packed, sketch_matrix, data))
    for k in sorted(range(1, data), key=lambda k: -min(k, data - k)):
        parts[k] = lax.ppermute(parts[k], "dp", [(i, (i + k) % data) for i in range(data)])
    return gather(parts)


def solution(mesh):
    in_specs = (
        P(("dp", "expert"), None),
        P(("dp", "expert"), None, None),
        P(("dp", "expert"), None),
        P(),
    )
    out_specs = (P("expert", None, "dp"), P("expert", None, "dp"))
    return jax.shard_map(shards, mesh=mesh, in_specs=in_specs, out_specs=out_specs, check_vma=False)
```
